128 devices in a mesh: dp: 32 (over z, y, core), ctx: 4 (over x).
Axes of the slice: x: 4, y: 4, z: 4, core: 2. Of those that a mesh axis runs over, the one named last changes fastest.
Arguments:
- tokens: bfloat16 [32, 1024, 1088], P('dp', 'ctx'), may hold values from -6 to 6
- cotangent: bfloat16 [32, 1024, 1088], P('dp', 'ctx'), may hold values from -12 to 12
- positions: int32 [32, 1024], P('dp', 'ctx'), may hold values from 0 to 1023, as said below
- w_qkv: float32 [1088, 3264], P('dp', 'ctx'), may hold values from -0.12126781 to 0.12126781
- w_out: float32 [1088, 1088], P('dp', 'ctx'), may hold values from -1.5 to 1.5
- w_up: float32 [1088, 4352], P('dp', 'ctx'), may hold values from -0.210096485 to 0.210096485
- w_down: float32 [4352, 1088], P('dp', 'ctx'), may hold values from -0.052599914 to 0.052599914
- vectors: float32 [1088, 12], P('dp', 'ctx'), may hold values from -1.2 to 4.2
- moment_qkv: float32 [1088, 3264], P('dp', 'ctx'), may hold values from -0.00018310547 to 0.00018310547
- square_qkv: float32 [1088, 3264], P('dp', 'ctx'), may hold values from 1.1235538e-11 to 4.5026628e-11
- moment_out: float32 [1088, 1088], P('dp', 'ctx'), may hold values from -6.1035156e-05 to 6.1035156e-05
- square_out: float32 [1088, 1088], P('dp', 'ctx'), may hold values from 1.5881812e-12 to 6.3358294e-12
- moment_up: float32 [1088, 4352], P('dp', 'ctx'), may hold values from -0.00030517578 to 0.00030517578
- square_up: float32 [1088, 4352], P('dp', 'ctx'), may hold values from 3.4466912e-11 to 1.3769869e-10
- moment_down: float32 [4352, 1088], P('dp', 'ctx'), may hold values from -0.00061035156 to 0.00061035156
- square_down: float32 [4352, 1088], P('dp', 'ctx'), may hold values from 1.5881813e-10 to 6.3358296e-10
- moment_vec: float32 [1088, 12], P('dp', 'ctx'), may hold values from -0.00036621094 to 0.00036621094
- square_vec: float32 [1088, 12], P('dp', 'ctx'), may hold values from 4.5026628e-11 to 1.7993755e-10
Outputs:
- outputs: bfloat16 [32, 1024, 1088], P('dp', 'ctx')
- d_tokens: float32 [32, 1024, 1088], P('dp', 'ctx')
- grad_norm: float32 [], replicated
- first_qkv: float32 [1088, 3264], P('dp', 'ctx')
- second_qkv: float32 [1088, 3264], P('dp', 'ctx')
- updated_qkv: float32 [1088, 3264], P('dp', 'ctx')
- first_out: float32 [1088, 1088], P('dp', 'ctx')
- second_out: float32 [1088, 1088], P('dp', 'ctx')
- updated_out: float32 [1088, 1088], P('dp', 'ctx')
- first_up: float32 [1088, 4352], P('dp', 'ctx')
- second_up: float32 [1088, 4352], P('dp', 'ctx')
- updated_up: float32 [1088, 4352], P('dp', 'ctx')
- first_down: float32 [4352, 1088], P('dp', 'ctx')
- second_down: float32 [4352, 1088], P('dp', 'ctx')
- updated_down: float32 [4352, 1088], P('dp', 'ctx')
- first_vec: float32 [1088, 12], P('dp', 'ctx')
- second_vec: float32 [1088, 12], P('dp', 'ctx')
- updated_vec: float32 [1088, 12], P('dp', 'ctx')
The draws below stay inside these ranges and needn't reach their ends.
Inputs may be any that keep to these rules, and one draw needn't show every extreme that they name: positions is 0 at the first token of every sequence and of every document and rises by one within a document; documents hold 200 to 2000 tokens, except the first and last of a sequence, which may be cut short.
All inputs are finite; a program needn't handle non-finite values.
Results may differ from the reference program's by a relative error of at most 0.013.
The reference program's roundings to bfloat16 on the way count: a program that leaves them out, or rounds other values in their place, can miss the bound.
Values may be sent and summed in bfloat16 or wider, within the bound.
No kernel may reach another device: no remote copies, remote signals or barrier semaphores. Data moves between devices by JAX's collectives and lax.ppermute only.
A program may use at most 192 MiB of HBM per device.

```python
import math
import jax
import jax.numpy as jnp
from jax import lax

HEADS = 17
HEAD_DIM = 64
D = 1088
FF = 4352
LEN = 1024
DOC_MIN = 200
DOC_MAX = 2000
STEP = 10
SHARD = 256
SEQS = 32


def rising(length, ceiling):
    return ceiling ** (jnp.arange(length, dtype=jnp.float32) / max(length - 1, 1))


def draw_cotangent(key, part):
    key = jax.random.fold_in(key, 11)
    extent = (SEQS, LEN, D)
    sample = jnp.clip(jax.random.normal(key, extent, jnp.float32), -4.0, 4.0)
    return (sample * rising(D, 3.0)).astype(jnp.bfloat16)


def draw_positions(key, part):
    key = jax.random.fold_in(key, 12)
    first_key, second_key, third_key, fourth_key = jax.random.split(key, 4)
    slot_count = LEN // DOC_MIN + 2
    opening = jax.random.randint(first_key, (SEQS, 1), 0, SHARD)
    longest = jax.random.randint(second_key, (SEQS, 1), LEN - SHARD + 1 - opening, DOC_MAX + 1)
    chosen = jax.random.randint(fourth_key, (), 0, SEQS)
    is_chosen = (jnp.arange(SEQS, dtype=jnp.int32) == chosen)[:, None]
    opening = jnp.where(is_chosen, 0, opening)
    longest = jnp.where(is_chosen, LEN, longest)
    others = jax.random.randint(third_key, (SEQS, slot_count), DOC_MIN, DOC_MAX + 1)
    later_starts = opening + longest + jnp.cumsum(others, axis=1)
    starts = jnp.concatenate([jnp.zeros((SEQS, 1), jnp.int32), opening, opening + longest, later_starts], axis=1)
    indices = jnp.arange(LEN, dtype=jnp.int32)
    latest = jnp.max(jnp.where(starts[:, None, :] <= indices[None, :, None], starts[:, None, :], 0), axis=2)
    return (indices[None, :] - latest).astype(jnp.int32)


def draw_w_qkv(key, part):
    key = jax.random.fold_in(key, 13)
    extent = (D, 3 * D)
    sample = jnp.clip(jax.random.normal(key, extent, jnp.float32), -4.0, 4.0)
    column = jnp.arange(3 * D)
    factor = jnp.where(column < 2 * D, 0.65, 1.0)
    return sample * factor[None, :] * D ** (-0.5)


def draw_w_up(key, part):
    key = jax.random.fold_in(key, 14)
    extent = (D, FF)
    sample = jnp.clip(jax.random.normal(key, extent, jnp.float32), -4.0, 4.0)
    return sample * jnp.sqrt(rising(FF, 3.0))[None, :] * D ** (-0.5)


def draw_w_down(key, part):
    key = jax.random.fold_in(key, 15)
    extent = (FF, D)
    sample = jnp.clip(jax.random.normal(key, extent, jnp.float32), -4.0, 4.0)
    return sample * jnp.sqrt(rising(FF, 3.0))[:, None] * 0.5 * FF ** (-0.5)


def draw_vectors(key, part):
    key = jax.random.fold_in(key, 16)
    extent = (D, 12)
    sample = jnp.clip(jax.random.normal(key, extent, jnp.float32), -4.0, 4.0)
    column = jnp.arange(12)
    gains = rising(D, 3.0)[:, None] * (1.0 + 0.1 * sample)
    shifts = 0.3 * sample
    is_gain = (column == 0) | (column == 5)
    return jnp.where(is_gain[None, :], gains, shifts)


def block_levels(key, shape, shards, least, largest):
    level, own = 1.0, jax.random.fold_in(key, 6)
    for axis_at, shards_of in shards:
        steps = jnp.exp(jax.random.uniform(jax.random.fold_in(own, axis_at), (shards_of,), jnp.float32, least / len(shards), largest / len(shards)))
        level = level * jnp.repeat(steps, shape[axis_at] // shards_of).reshape([-1 if axis == axis_at else 1 for axis in range(len(shape))])
    return level


def normal_values(rng, shape, width, reach, cuts=(), held_as=jnp.bfloat16):
    loudness = block_levels(rng, shape, cuts, -0.22, 0.18) if cuts else 1.0
    values = jax.random.normal(rng, shape, jnp.float32) * width * loudness
    return jnp.minimum(jnp.maximum(values, -reach), reach).astype(held_as)


def setup_inputs(seed: int = 0) -> dict:
    splits = jax.random.split(jax.random.key(seed), 19)
    return {
        "tokens": normal_values(splits[0], (SEQS, LEN, D), 1.0, 6.0, ((0, 32), (1, 4))),
        "cotangent": draw_cotangent(jax.random.fold_in(splits[18], 71), 0),
        "positions": draw_positions(jax.random.fold_in(splits[18], 71), 0),
        "w_qkv": draw_w_qkv(jax.random.fold_in(splits[18], 71), 0),
        "w_out": normal_values(splits[4], (D, D), (max(1, D * 16 // LEN)) ** -0.5, 1.5, ((0, 32), (1, 4)), jnp.float32),
        "w_up": draw_w_up(jax.random.fold_in(splits[18], 71), 0),
        "w_down": draw_w_down(jax.random.fold_in(splits[18], 71), 0),
        "vectors": draw_vectors(jax.random.fold_in(splits[18], 71), 0),
        "moment_qkv": normal_values(splits[8], (D, 3 * D), (0.0128 * D ** -1.0), 0.00018310547, ((0, 32), (1, 4)), jnp.float32),
        "square_qkv": jnp.clip(jnp.exp(math.log(4.502662825922599e-11) - 1.3881723 * jax.random.uniform(splits[9], (D, 3 * D), jnp.float32) ** block_levels(splits[9], (D, 3 * D), ((0, 32), (1, 4)), -0.2, 0.2)), 1.1235537673848217e-11, 4.502662825922599e-11),
        "moment_out": normal_values(splits[10], (D, D), (0.0048 * D ** -1.0), 6.103515625e-05, ((0, 32), (1, 4)), jnp.float32),
        "square_out": jnp.clip(jnp.exp(math.log(6.335829430548223e-12) - 1.38363128 * jax.random.uniform(splits[11], (D, D), jnp.float32) ** block_levels(splits[11], (D, D), ((0, 32), (1, 4)), -0.2, 0.2)), 1.5881811924606248e-12, 6.335829430548223e-12),
        "moment_up": normal_values(splits[12], (D, FF), (0.0224 * D ** -1.0), 0.00030517578, ((0, 32), (1, 4)), jnp.float32),
        "square_up": jnp.clip(jnp.exp(math.log(1.3769868578705768e-10) - 1.385068 * jax.random.uniform(splits[13], (D, FF), jnp.float32) ** block_levels(splits[13], (D, FF), ((0, 32), (1, 4)), -0.2, 0.2)), 3.4466911963404456e-11, 1.3769868578705768e-10),
        "moment_down": normal_values(splits[14], (FF, D), (0.048 * D ** -1.0), 0.00061035156, ((0, 32), (1, 4)), jnp.float32),
        "square_down": jnp.clip(jnp.exp(math.log(6.33582963871504e-10) - 1.38363127 * jax.random.uniform(splits[15], (FF, D), jnp.float32) ** block_levels(splits[15], (FF, D), ((0, 32), (1, 4)), -0.2, 0.2)), 1.5881812531759465e-10, 6.33582963871504e-10),
        "moment_vec": normal_values(splits[16], (D, 12), (0.0256 * D ** -1.0), 0.00036621094, ((0, 32), (1, 4)), jnp.float32),
        "square_vec": jnp.clip(jnp.exp(math.log(1.799375509703438e-10) - 1.3853558 * jax.random.uniform(splits[17], (D, 12), jnp.float32) ** block_levels(splits[17], (D, 12), ((0, 32), (1, 4)), -0.2, 0.2)), 4.502662825922599e-11, 1.799375509703438e-10),
    }


PRECISE = lax.Precision.HIGHEST
NORM_EPS = 1e-05
ADAM_EPS = 1e-08
BETA_FIRST = 0.9
BETA_SECOND = 0.999
CLIP_LIMIT = 1.0
GELU_SCALE = 0.7978845608
GELU_CUBIC = 0.044715
MASK_FILL = -1e+30
LEARN_RATES = (0.05, 0.5, 0.1, 0.03, 1.0)
WEIGHT_DECAYS = (0.1, 0.1, 0.1, 0.1, 0.0)

@jax.custom_vjp
def low(v):
    return lax.optimization_barrier(v.astype(jnp.bfloat16)).astype(jnp.float32)

@jax.custom_vjp
def low_back(v):
    return v

def low_keep(v):
    return (low(v), None)

def low_pass(kept, grad):
    return (grad,)

def back_keep(v):
    return (v, None)

def back_low(kept, grad):
    return (low(grad),)
low.defvjp(low_keep, low_pass)
low_back.defvjp(back_keep, back_low)

def layer_norm(inputs, gain_col, shift_col):
    centre = inputs - lax.optimization_barrier(jnp.mean(inputs, axis=-1, keepdims=True))
    spread = lax.optimization_barrier(jnp.mean(centre * centre, axis=-1, keepdims=True))
    return centre * lax.rsqrt(spread + NORM_EPS) * gain_col + shift_col

def gelu(inputs):
    inner = GELU_SCALE * (inputs + GELU_CUBIC * inputs * inputs * inputs)
    return 0.5 * inputs * (1.0 + jnp.tanh(inner))

def adam_step(weight, moment, square, gradient, rate, decay):
    first = BETA_FIRST * moment + (1.0 - BETA_FIRST) * gradient
    second = BETA_SECOND * square + (1.0 - BETA_SECOND) * gradient * gradient
    first_hat = first / (1.0 - BETA_FIRST ** STEP)
    second_hat = second / (1.0 - BETA_SECOND ** STEP)
    updated = weight - rate * (first_hat / (jnp.sqrt(second_hat) + ADAM_EPS) + decay * weight)
    return (first, second, updated)

def split_heads(inputs):
    return inputs.reshape(LEN, HEADS, HEAD_DIM).transpose(1, 0, 2)

def forward(seq_tokens, seq_pos, w_qkv, w_out, w_up, w_down, vectors):
    qkv_low = low(w_qkv)
    out_low = low(w_out)
    up_low = low(w_up)
    down_low = low(w_down)
    vec_low = low(vectors)
    norm_one = layer_norm(seq_tokens, vec_low[:, 0], vec_low[:, 1])
    qkv_all = jnp.dot(low(norm_one), qkv_low, precision=PRECISE)
    queries = low_back(low(qkv_all[:, :D] + vec_low[:, 2]))
    keys_all = low_back(low(qkv_all[:, D:2 * D]))
    values_all = low_back(low(qkv_all[:, 2 * D:] + vec_low[:, 3]))
    indices = jnp.arange(LEN, dtype=jnp.int32)
    allowed = (indices[None, :] <= indices[:, None]) & (indices[None, :] >= (indices - seq_pos)[:, None])
    head_scale = HEAD_DIM ** (-0.5)

    def one_head(head_items):
        query_h, key_h, value_h = head_items
        raw_scores = jnp.dot(query_h, key_h.T, precision=PRECISE)
        scores = jnp.where(allowed, low_back(raw_scores * head_scale), MASK_FILL)
        row_peak = lax.optimization_barrier(jnp.max(scores, axis=-1, keepdims=True))
        exp_terms = jnp.exp(scores - row_peak)
        probabilities = exp_terms / lax.optimization_barrier(jnp.sum(exp_terms, axis=-1, keepdims=True))
        return jnp.dot(low(probabilities), value_h, precision=PRECISE)
    per_head = lax.map(jax.checkpoint(one_head), (split_heads(queries), split_heads(keys_all), split_heads(values_all)))
    heads = low_back(low(per_head.transpose(1, 0, 2).reshape(LEN, D)))
    mixed = seq_tokens + low_back(jnp.dot(heads, out_low, precision=PRECISE) + vec_low[:, 4])
    norm_two = layer_norm(mixed, vec_low[:, 5], vec_low[:, 6])
    up_bias = vec_low[:, 7:7 + FF // D].T.reshape(FF)
    pre_act = low_back(jnp.dot(low(norm_two), up_low, precision=PRECISE) + up_bias)
    act_low = low(gelu(pre_act))
    return mixed + low_back(jnp.dot(act_low, down_low, precision=PRECISE) + vec_low[:, 11])

def reference(tokens, cotangent, positions, w_qkv, w_out, w_up, w_down, vectors, moment_qkv, square_qkv, moment_out, square_out, moment_up, square_up, moment_down, square_down, moment_vec, square_vec):
    masters = (w_qkv, w_out, w_up, w_down, vectors)

    def one_sequence(running, batch_item):
        seq_tokens, seq_cot, seq_pos = batch_item

        def local_forward(inputs, weight_qkv, weight_out, weight_up, weight_down, weight_vec):
            return forward(inputs, seq_pos, weight_qkv, weight_out, weight_up, weight_down, weight_vec)
        result, pull_back = jax.vjp(local_forward, seq_tokens.astype(jnp.float32), masters[0], masters[1], masters[2], masters[3], masters[4])
        grads = pull_back(seq_cot.astype(jnp.float32))
        running = jax.tree.map(jnp.add, running, tuple(grads[1:]))
        return (running, (result.astype(jnp.bfloat16), grads[0]))
    starting = jax.tree.map(jnp.zeros_like, masters)
    totals, (outputs, d_tokens) = lax.scan(one_sequence, starting, (tokens, cotangent, positions))
    total_sq = jnp.zeros((), jnp.float32)
    for gradient in totals:
        total_sq = total_sq + jnp.sum(gradient * gradient)
    grad_norm = jnp.sqrt(total_sq)
    clip_factor = CLIP_LIMIT / jnp.maximum(grad_norm, CLIP_LIMIT)
    first_qkv, second_qkv, updated_qkv = adam_step(w_qkv, moment_qkv, square_qkv, totals[0] * clip_factor, LEARN_RATES[0], WEIGHT_DECAYS[0])
    first_out, second_out, updated_out = adam_step(w_out, moment_out, square_out, totals[1] * clip_factor, LEARN_RATES[1], WEIGHT_DECAYS[1])
    first_up, second_up, updated_up = adam_step(w_up, moment_up, square_up, totals[2] * clip_factor, LEARN_RATES[2], WEIGHT_DECAYS[2])
    first_down, second_down, updated_down = adam_step(w_down, moment_down, square_down, totals[3] * clip_factor, LEARN_RATES[3], WEIGHT_DECAYS[3])
    first_vec, second_vec, updated_vec = adam_step(vectors, moment_vec, square_vec, totals[4] * clip_factor, LEARN_RATES[4], WEIGHT_DECAYS[4])
    return (outputs, d_tokens, grad_norm, first_qkv, second_qkv, updated_qkv, first_out, second_out, updated_out, first_up, second_up, updated_up, first_down, second_down, updated_down, first_vec, second_vec, updated_vec)
```

```python
import jax
import jax.numpy as jnp
from jax import lax
from jax.experimental import pallas as pl
from jax.experimental.pallas import tpu as pltpu
from jax.sharding import PartitionSpec as P

HEADS = 17
HEAD_DIM = 64
SLOTS = 5
GROUP = 4 * HEAD_DIM
SPAN = SLOTS * HEAD_DIM
STEP = 10

NORM_EPS = 1e-05
ADAM_EPS = 1e-08
BETA_FIRST = 0.9
BETA_SECOND = 0.999
CLIP_LIMIT = 1.0
GELU_SCALE = 0.7978845608
GELU_CUBIC = 0.044715
MASK_FILL = -1e30
LEARN_RATES = (0.05, 0.5, 0.1, 0.03, 1.0)
WEIGHT_DECAYS = (0.1, 0.1, 0.1, 0.1, 0.0)

LOW = jnp.bfloat16
FULL = jnp.float32
RING = 4
CORES = 2


def layer_norm(inputs, gain_col, shift_col):
    centre = inputs - jnp.mean(inputs, axis=-1, keepdims=True)
    spread = jnp.mean(centre * centre, axis=-1, keepdims=True)
    return centre * lax.rsqrt(spread + NORM_EPS) * gain_col + shift_col


def gelu(inputs):
    inner = GELU_SCALE * (inputs + GELU_CUBIC * inputs * inputs * inputs)
    return 0.5 * inputs * (1.0 + jnp.tanh(inner))


def adam_step(weight, moment, square, gradient, rate, decay):
    first = BETA_FIRST * moment + (1.0 - BETA_FIRST) * gradient
    second = BETA_SECOND * square + (1.0 - BETA_SECOND) * gradient * gradient
    first_hat = first / (1.0 - BETA_FIRST**STEP)
    second_hat = second / (1.0 - BETA_SECOND**STEP)
    updated = weight - rate * (first_hat / (jnp.sqrt(second_hat) + ADAM_EPS) + decay * weight)
    return (first, second, updated)


def dot(left, right):
    return jnp.dot(left, right, preferred_element_type=FULL)


def dot_last(left, right):
    return lax.dot_general(left, right, (((1,), (1,)), ((), ())), preferred_element_type=FULL)


def dot_first(left, right):
    return lax.dot_general(left, right, (((0,), (0,)), ((), ())), preferred_element_type=FULL)


def block_at(rank, index):
    return lax.rem(index + RING - rank, RING)


def bias_of(pos_row, query_block, key_block, length):
    keys = key_block * length + lax.broadcasted_iota(jnp.int32, (length, length), 0)
    queries = query_block * length + lax.broadcasted_iota(jnp.int32, (length, length), 1)
    allowed = (keys <= queries) & (keys >= queries - pos_row)
    return jnp.where(allowed, 0.0, MASK_FILL)


def head_cols(part, slot):
    first = part * SPAN + slot * HEAD_DIM
    return slice(first, first + HEAD_DIM)


def attend_forward(rank_ref, pos_ref, qkv_ref, heads_ref, lse_ref, turned_ref):
    rank = rank_ref[0]
    length = qkv_ref.shape[1]
    scale = HEAD_DIM ** (-0.5)
    for key_block in range(RING):
        at = block_at(rank, key_block)
        turned_ref[key_block] = qkv_ref[at, :, 2 * SPAN : 3 * SPAN].T
    for query_block in range(RING):
        at = block_at(rank, query_block)
        pos_row = pos_ref[at]
        biases = [bias_of(pos_row, query_block, k, length) for k in range(query_block + 1)]
        columns = []
        for slot in range(SLOTS):
            query = qkv_ref[at, :, head_cols(0, slot)] * jnp.asarray(scale, LOW)
            scores = [
                dot_last(qkv_ref[block_at(rank, k), :, head_cols(1, slot)], query) + biases[k]
                for k in range(query_block + 1)
            ]
            peak = jnp.max(scores[0], axis=0, keepdims=True)
            for part in scores[1:]:
                peak = jnp.maximum(peak, jnp.max(part, axis=0, keepdims=True))
            terms = [jnp.exp(part - peak) for part in scores]
            total = jnp.sum(terms[0], axis=0, keepdims=True)
            for part in terms[1:]:
                total = total + jnp.sum(part, axis=0, keepdims=True)
            inverse = 1.0 / total
            result = None
            for k in range(query_block + 1):
                value = turned_ref[k, slot * HEAD_DIM : (slot + 1) * HEAD_DIM, :]
                term = dot(value, (terms[k] * inverse).astype(LOW))
                result = term if result is None else result + term
            columns.append(result)
            lse_ref[at, slot : slot + 1, :] = peak + jnp.log(total)
        heads_ref[at] = jnp.concatenate(columns, axis=0).T.astype(LOW)


def attend_backward(
    rank_ref, pos_ref, qkv_ref, grad_ref, lse_ref, out_ref, turned_ref, bias_ref
):
    rank = rank_ref[0]
    length = qkv_ref.shape[1]
    scale = HEAD_DIM ** (-0.5)
    pairs = [(q, k) for q in range(RING) for k in range(q + 1)]
    for key_block in range(RING):
        turned_ref[key_block] = qkv_ref[block_at(rank, key_block), :, SPAN : 2 * SPAN].T
    for number, (q, k) in enumerate(pairs):
        bias_ref[number] = bias_of(pos_ref[block_at(rank, q)], q, k, length)
    for slot in range(SLOTS):
        rows = slice(slot * HEAD_DIM, (slot + 1) * HEAD_DIM)
        keys = [qkv_ref[block_at(rank, k), :, head_cols(1, slot)] for k in range(RING)]
        values = [qkv_ref[block_at(rank, k), :, head_cols(2, slot)] for k in range(RING)]
        d_keys = [None] * RING
        d_values = [None] * RING
        if slot == SLOTS - 1:
            keep = jnp.where(rank == RING - 1, 1.0, 0.0)
        else:
            keep = None

        def finish(item):
            return (item if keep is None else item * keep).astype(LOW)

        for q in range(RING):
            at = block_at(rank, q)
            query = qkv_ref[at, :, head_cols(0, slot)] * jnp.asarray(scale, LOW)
            grad = grad_ref[at, :, rows]
            lse = lse_ref[at, slot : slot + 1, :]
            probs = []
            d_probs = []
            inner = None
            for k in range(q + 1):
                score = dot_last(keys[k], query) + bias_ref[pairs.index((q, k))]
                prob = jnp.exp(score - lse)
                d_prob = dot_last(values[k], grad)
                term = jnp.sum(prob * d_prob, axis=0, keepdims=True)
                inner = term if inner is None else inner + term
                probs.append(prob)
                d_probs.append(d_prob)
            d_query = None
            for k in range(q + 1):
                d_score = (probs[k] * (d_probs[k] - inner)).astype(LOW)
                d_key = dot(d_score, query)
                d_value = dot(probs[k].astype(LOW), grad)
                term = dot(turned_ref[k, rows, :], d_score)
                d_keys[k] = d_key if d_keys[k] is None else d_keys[k] + d_key
                d_values[k] = d_value if d_values[k] is None else d_values[k] + d_value
                d_query = term if d_query is None else d_query + term
            out_ref[at, :, head_cols(0, slot)] = finish(d_query.T * scale)
        for k in range(RING):
            at = block_at(rank, k)
            out_ref[at, :, head_cols(1, slot)] = finish(d_keys[k])
            out_ref[at, :, head_cols(2, slot)] = finish(d_values[k])


VMEM_SPEC = pl.BlockSpec(memory_space=pltpu.VMEM)
SMEM_SPEC = pl.BlockSpec(memory_space=pltpu.SMEM)
KERNEL_PARAMS = pltpu.CompilerParams(vmem_limit_bytes=48 * 1024 * 1024)


def run_forward(rank, pos, qkv):
    blocks, length, unused = qkv.shape
    return pl.pallas_call(
        attend_forward,
        out_shape=(
            jax.ShapeDtypeStruct((blocks, length, SPAN), LOW),
            jax.ShapeDtypeStruct((blocks, 8, length), FULL),
        ),
        in_specs=[SMEM_SPEC, VMEM_SPEC, VMEM_SPEC],
        out_specs=(VMEM_SPEC, VMEM_SPEC),
        scratch_shapes=[pltpu.VMEM((blocks, SPAN, length), LOW)],
        compiler_params=KERNEL_PARAMS,
        cost_estimate=pl.CostEstimate(
            flops=2 * 2 * 10 * 256 * 256 * SPAN, bytes_accessed=4 << 20, transcendentals=3 << 20
        ),
    )(rank, pos, qkv)


def run_backward(rank, pos, qkv, grads, lse):
    blocks, length, width = qkv.shape
    return pl.pallas_call(
        attend_backward,
        out_shape=jax.ShapeDtypeStruct((blocks, length, width), LOW),
        in_specs=[SMEM_SPEC, VMEM_SPEC, VMEM_SPEC, VMEM_SPEC, VMEM_SPEC],
        out_specs=VMEM_SPEC,
        scratch_shapes=[
            pltpu.VMEM((blocks, SPAN, length), LOW),
            pltpu.VMEM((10, length, length), FULL),
        ],
        compiler_params=KERNEL_PARAMS,
        cost_estimate=pl.CostEstimate(
            flops=2 * 5 * 10 * 256 * 256 * SPAN, bytes_accessed=8 << 20, transcendentals=3 << 20
        ),
    )(rank, pos, qkv, grads, lse)


def ctx_shift(item, step):
    return lax.ppermute(item, "ctx", [(i, (i + step) % RING) for i in range(RING)])


def gather_relative(item):
    half = item.shape[0] // 2
    left = ctx_shift(item, 1)
    right = ctx_shift(item, 3)
    top = ctx_shift(left[:half], 1)
    bottom = ctx_shift(right[half:], 3)
    return jnp.concatenate([item, right, top, bottom, left], axis=0)


def gather_small(item):
    return jnp.stack([item, ctx_shift(item, 3), ctx_shift(item, 2), ctx_shift(item, 1)])


def to_global(relative, rank):
    doubled = jnp.concatenate([relative, relative[: RING - 1]], axis=0)
    return lax.dynamic_slice_in_dim(doubled, lax.rem(RING - rank, RING), RING, axis=0)


def exchange(pieces):
    return [pieces[0]] + [ctx_shift(pieces[RING - r], RING - r) for r in (1, 2, 3)]


def reduce_ctx(partial):
    length = partial.shape[0] // RING
    own = partial[:length]
    others = partial[length:].astype(LOW)
    arrived = [
        ctx_shift(others[(r - 1) * length : r * length], r).astype(FULL) for r in (1, 2, 3)
    ]
    return own + (arrived[0] + arrived[1] + arrived[2])


def dp_perm(dp_count, move):
    rows = dp_count // (RING * CORES)
    pairs = []
    for z in range(RING):
        for y in range(rows):
            for core in range(CORES):
                to_z, to_y, to_core = move(z, y, core, rows)
                pairs.append(((z * rows + y) * CORES + core, (to_z * rows + to_y) * CORES + to_core))
    return pairs


def reduce_dp(grad, rank_z, rank_y, rank_core, order):
    dp_count = grad.shape[0] * grad.shape[1] * grad.shape[2]
    other = lax.dynamic_index_in_dim(grad, 1 - rank_core, 2, keepdims=False).astype(LOW)
    own = lax.dynamic_index_in_dim(grad, rank_core, 2, keepdims=False)
    swap = dp_perm(dp_count, lambda z, y, core, rows: (z, y, 1 - core))
    total = own.astype(FULL) + lax.ppermute(other, "dp", swap).astype(FULL)
    for name in order:
        axis = 0 if (name == "z" or order[0] == "z") else 1
        size = total.shape[axis]
        at = rank_z if name == "z" else rank_y
        low = total.astype(LOW)
        result = lax.dynamic_index_in_dim(total, at, axis, keepdims=False)
        for step in range(1, size):
            piece = lax.dynamic_index_in_dim(low, lax.rem(at + step, size), axis, keepdims=False)
            if name == "z":
                perm = dp_perm(dp_count, lambda z, y, core, rows: ((z + step) % RING, y, core))
            else:
                perm = dp_perm(dp_count, lambda z, y, core, rows: (z, (y + step) % rows, core))
            result = result + lax.ppermute(piece, "dp", perm).astype(FULL)
        total = result
    return total


def sum_everywhere(item, dp_count):
    rows = dp_count // (RING * CORES)
    swap = dp_perm(dp_count, lambda z, y, core, rows: (z, y, 1 - core))
    item = item + lax.ppermute(item, "dp", swap)
    for name in ("y", "z", "x"):
        parts = [item]
        for step in (1, 2, 3):
            if name == "x":
                perm = [(i, i ^ step) for i in range(RING)]
                parts.append(lax.ppermute(item, "ctx", perm))
            elif name == "z":
                perm = dp_perm(dp_count, lambda z, y, core, rows: (z ^ step, y, core))
                parts.append(lax.ppermute(item, "dp", perm))
            elif rows == RING:
                perm = dp_perm(dp_count, lambda z, y, core, rows: (z, y ^ step, core))
                parts.append(lax.ppermute(item, "dp", perm))
        if len(parts) == RING:
            item = (parts[0] + parts[1]) + (parts[2] + parts[3])
    return item


def swap_planes(item, dp_count):
    inner = dp_count // RING
    pairs = [
        ((z * inner + rest) * RING + x, (x * inner + rest) * RING + z)
        for z in range(RING)
        for rest in range(inner)
        for x in range(RING)
    ]
    return lax.ppermute(item, ("dp", "ctx"), pairs)


def body(
    tokens,
    cotangent,
    positions,
    w_qkv,
    w_out,
    w_up,
    w_down,
    vectors,
    moment_qkv,
    square_qkv,
    moment_out,
    square_out,
    moment_up,
    square_up,
    moment_down,
    square_down,
    moment_vec,
    square_vec,
):
    unused, local_len, width = tokens.shape
    dp_count = lax.axis_size("dp")
    rows_y = dp_count // (RING * CORES)
    rank = lax.axis_index("ctx")
    dp_rank = lax.axis_index("dp")
    rank_core = lax.rem(dp_rank, CORES)
    rank_y = lax.rem(lax.div(dp_rank, CORES), rows_y)
    rank_z = lax.div(dp_rank, CORES * rows_y)
    row_size = w_qkv.shape[0]
    full_len = local_len * RING

    shard_cols = jnp.concatenate(
        [w_qkv.astype(LOW), w_out.astype(LOW), vectors.astype(LOW)], axis=1
    )
    gathered = to_global(gather_small(shard_cols), rank)
    qkv_size, out_size = w_qkv.shape[1], w_out.shape[1]
    qkv_rows = jnp.concatenate([gathered[s, :, :qkv_size] for s in range(RING)], axis=1)
    out_rows = jnp.concatenate(
        [gathered[s, :, qkv_size : qkv_size + out_size] for s in range(RING)], axis=1
    )
    vec_rows = jnp.concatenate([gathered[s, :, qkv_size + out_size :] for s in range(RING)], axis=1)
    head_start = rank * GROUP
    qkv_own = [
        lax.dynamic_slice_in_dim(qkv_rows[:, part * width : (part + 1) * width], head_start, SPAN, 1)
        for part in range(3)
    ]
    first_all = lax.all_gather(
        jnp.concatenate(qkv_own + [vec_rows], axis=1), "dp", axis=0, tiled=True
    )
    down_swapped = swap_planes(w_down.astype(LOW), dp_count)
    down_shape = down_swapped.shape
    second_all = lax.all_gather(
        jnp.concatenate(
            [out_rows, w_up.astype(LOW), down_swapped.reshape(row_size, width)], axis=1
        ),
        "dp",
        axis=0,
        tiled=False,
    )
    qkv_low = first_all[:, : 3 * SPAN]
    vec_full = first_all[:, 3 * SPAN :].astype(FULL)
    out_low = second_all[:, :, :width].reshape(width, width)
    up_low = second_all[:, :, width : 2 * width].reshape(width, width)
    down_low = (
        second_all[:, :, 2 * width :]
        .reshape(RING, dp_count // RING * down_shape[0], down_shape[1])
        .transpose(1, 0, 2)
        .reshape(width, width)
    )

    token_low = tokens.reshape(local_len, width)
    cot_low = cotangent.reshape(local_len, width)
    token_seq = gather_relative(token_low)
    pos_seq = gather_small(positions)
    cot_seq = gather_relative(cot_low)
    rank_arg = rank.astype(jnp.int32).reshape(1)

    a_one = layer_norm(token_seq.astype(FULL), vec_full[:, 0], vec_full[:, 1]).astype(LOW)
    q_bias = lax.dynamic_slice_in_dim(vec_full[:, 2], head_start, SPAN, 0)
    v_bias = lax.dynamic_slice_in_dim(vec_full[:, 3], head_start, SPAN, 0)
    qkv_bias = jnp.concatenate([q_bias, jnp.zeros_like(q_bias), v_bias])
    qkv_seq = (dot(a_one, qkv_low) + qkv_bias).astype(LOW)
    qkv_blocks = qkv_seq.reshape(RING, local_len, 3 * SPAN)
    heads_blocks, lse = run_forward(rank_arg, pos_seq, qkv_blocks)

    came = exchange([heads_blocks[r] for r in range(RING)])
    by_group = to_global(jnp.stack(came), rank)
    heads_low = jnp.concatenate(
        [by_group[s, :, :GROUP] for s in range(RING - 1)] + [by_group[RING - 1]], axis=1
    )
    inputs = token_low.astype(FULL)
    mixed = inputs + (dot(heads_low, out_low) + vec_full[:, 4])
    a_two = layer_norm(mixed, vec_full[:, 5], vec_full[:, 6]).astype(LOW)
    a_two_seq = gather_relative(a_two)
    up_bias = lax.dynamic_index_in_dim(vec_full, 7 + rank, 1, keepdims=False)
    d_act = dot_last(cot_seq, down_low)
    pre_act = dot(a_two_seq, up_low) + up_bias
    act, gelu_pull = jax.vjp(gelu, pre_act)
    act_low = act.astype(LOW)
    d_pre = gelu_pull(d_act)[0].astype(LOW)
    d_two = reduce_ctx(dot_last(d_pre, up_low))
    down_sum = reduce_ctx(dot(act_low, down_low))
    outputs = (mixed + (down_sum + vec_full[:, 11])).astype(LOW).reshape(tokens.shape)

    unused, second_pull = jax.vjp(layer_norm, mixed, vec_full[:, 5], vec_full[:, 6])
    d_mixed_part, d_gain_two, d_shift_two = second_pull(d_two)
    cot_full = cot_low.astype(FULL)
    d_mixed = cot_full + d_mixed_part
    d_branch = d_mixed.astype(LOW)
    d_heads = dot_last(d_branch, out_low).astype(LOW)
    pieces = [
        lax.dynamic_slice_in_dim(d_heads, lax.rem(rank + r, RING) * GROUP, SPAN, 1)
        for r in range(RING)
    ]
    d_heads_blocks = jnp.stack(exchange(pieces))
    d_qkv_blocks = run_backward(rank_arg, pos_seq, qkv_blocks, d_heads_blocks, lse)
    d_qkv = d_qkv_blocks.reshape(full_len, 3 * SPAN)

    def summed(grad, order):
        return reduce_dp(grad, rank_z, rank_y, rank_core, order)

    lead = (RING, rows_y, CORES)
    grad_up = summed(
        dot_first(a_two_seq, d_pre).astype(LOW).reshape(lead + (row_size, width)), ("y", "z")
    )
    grad_down_part = (
        dot_first(act_low, cot_seq)
        .astype(LOW)
        .reshape(rows_y, CORES, down_shape[0], RING, down_shape[1])
        .transpose(3, 0, 1, 2, 4)
    )
    grad_down = swap_planes(summed(grad_down_part, ("z", "y")), dp_count)
    grad_out_part = dot_first(heads_low, d_branch).astype(LOW)
    out_pieces = [
        lax.dynamic_slice_in_dim(grad_out_part, lax.rem(rank + r, RING) * out_size, out_size, 1)
        for r in range(RING)
    ]
    out_came = exchange(out_pieces)
    grad_out_cols = (
        (out_came[0].astype(FULL) + out_came[1].astype(FULL))
        + (out_came[2].astype(FULL) + out_came[3].astype(FULL))
    ).astype(LOW)
    grad_out = summed(grad_out_cols.reshape(lead + (row_size, out_size)), ("y", "z"))
    grad_qkv_part = dot_first(a_one, d_qkv).astype(LOW).reshape(lead + (row_size, 3 * SPAN))
    split = 512
    grad_qkv_own = jnp.concatenate(
        [
            summed(grad_qkv_part[..., :split], ("y", "z")),
            summed(grad_qkv_part[..., split:], ("z", "y")),
        ],
        axis=1,
    )
    d_one = reduce_ctx(dot_last(d_qkv, qkv_low))
    unused, first_pull = jax.vjp(layer_norm, inputs, vec_full[:, 0], vec_full[:, 1])
    d_input_part, d_gain_one, d_shift_one = first_pull(d_one)
    d_tokens = (d_mixed + d_input_part).reshape(tokens.shape)

    d_qkv_sums = jnp.sum(d_qkv.astype(FULL), axis=0)
    empty = jnp.zeros((width,), FULL)
    d_pre_sums = jnp.sum(d_pre.astype(FULL), axis=0)
    vec_terms = jnp.stack(
        [
            d_gain_one,
            d_shift_one,
            lax.dynamic_update_slice(empty, d_qkv_sums[:SPAN], (head_start,)),
            lax.dynamic_update_slice(empty, d_qkv_sums[2 * SPAN :], (head_start,)),
            jnp.sum(d_branch.astype(FULL), axis=0),
            d_gain_two,
            d_shift_two,
        ]
        + [jnp.where(rank == c, d_pre_sums, 0.0) for c in range(RING)]
        + [jnp.sum(cot_full, axis=0)],
        axis=0,
    )
    local_sq = (
        jnp.sum(grad_qkv_own * grad_qkv_own)
        + jnp.sum(grad_out * grad_out)
        + jnp.sum(grad_up * grad_up)
        + jnp.sum(grad_down * grad_down)
    )
    vec_count = vec_terms.shape[0]
    payload = jnp.concatenate(
        [
            vec_terms,
            jnp.where(lax.broadcasted_iota(jnp.int32, (4, width), 1) == 0, local_sq, 0.0)
            * jnp.where(lax.broadcasted_iota(jnp.int32, (4, width), 0) == 0, 1.0, 0.0),
        ],
        axis=0,
    )
    payload = sum_everywhere(payload, dp_count)
    vec_total = payload[:vec_count]
    total_sq = payload[vec_count, 0] + jnp.sum(vec_total * vec_total)
    grad_norm = jnp.sqrt(total_sq)
    clip_factor = CLIP_LIMIT / jnp.maximum(grad_norm, CLIP_LIMIT)

    col_size = vec_count // RING
    grad_vec = lax.dynamic_slice(
        vec_total, (rank * col_size, dp_rank * row_size), (col_size, row_size)
    ).T
    qkv_groups = to_global(gather_small(grad_qkv_own), rank)
    grad_qkv_rows = jnp.concatenate(
        [
            qkv_groups[s, :, part * SPAN : part * SPAN + (SPAN if s == RING - 1 else GROUP)]
            for part in range(3)
            for s in range(RING)
        ],
        axis=1,
    )
    grad_qkv = lax.dynamic_slice_in_dim(grad_qkv_rows, rank * qkv_size, qkv_size, 1)

    first_qkv, second_qkv, updated_qkv = adam_step(
        w_qkv, moment_qkv, square_qkv, grad_qkv * clip_factor, LEARN_RATES[0], WEIGHT_DECAYS[0]
    )
    first_out, second_out, updated_out = adam_step(
        w_out, moment_out, square_out, grad_out * clip_factor, LEARN_RATES[1], WEIGHT_DECAYS[1]
    )
    first_up, second_up, updated_up = adam_step(
        w_up, moment_up, square_up, grad_up * clip_factor, LEARN_RATES[2], WEIGHT_DECAYS[2]
    )
    first_down, second_down, updated_down = adam_step(
        w_down, moment_down, square_down, grad_down * clip_factor, LEARN_RATES[3], WEIGHT_DECAYS[3]
    )
    first_vec, second_vec, updated_vec = adam_step(
        vectors, moment_vec, square_vec, grad_vec * clip_factor, LEARN_RATES[4], WEIGHT_DECAYS[4]
    )
    return (
        outputs,
        d_tokens,
        grad_norm,
        first_qkv,
        second_qkv,
        updated_qkv,
        first_out,
        second_out,
        updated_out,
        first_up,
        second_up,
        updated_up,
        first_down,
        second_down,
        updated_down,
        first_vec,
        second_vec,
        updated_vec,
    )


def solution(mesh):
    token_spec = P("dp", "ctx", None)
    flat_spec = P("dp", "ctx")
    return jax.shard_map(
        body,
        mesh=mesh,
        in_specs=(token_spec, token_spec) + (flat_spec,) * 16,
        out_specs=(token_spec, token_spec, P()) + (flat_spec,) * 15,
        check_vma=False,
    )
```

```python
import jax
import jax.numpy as jnp
from jax import lax
from jax.experimental import pallas as pl
from jax.experimental.pallas import tpu as pltpu
from jax.sharding import PartitionSpec as P

HEADS = 17
HEAD_DIM = 64
SLOTS = 5
GROUP = 4 * HEAD_DIM
SPAN = SLOTS * HEAD_DIM
STEP = 10

NORM_EPS = 1e-05
ADAM_EPS = 1e-08
BETA_FIRST = 0.9
BETA_SECOND = 0.999
CLIP_LIMIT = 1.0
GELU_SCALE = 0.7978845608
GELU_CUBIC = 0.044715
MASK_FILL = -1e30
LEARN_RATES = (0.05, 0.5, 0.1, 0.03, 1.0)
WEIGHT_DECAYS = (0.1, 0.1, 0.1, 0.1, 0.0)

LOW = jnp.bfloat16
FULL = jnp.float32
RING = 4
CORES = 2


def layer_norm(inputs, gain_col, shift_col):
    centre = inputs - jnp.mean(inputs, axis=-1, keepdims=True)
    spread = jnp.mean(centre * centre, axis=-1, keepdims=True)
    return centre * lax.rsqrt(spread + NORM_EPS) * gain_col + shift_col


def gelu(inputs):
    inner = GELU_SCALE * (inputs + GELU_CUBIC * inputs * inputs * inputs)
    return 0.5 * inputs * (1.0 + jnp.tanh(inner))


def adam_step(weight, moment, square, gradient, rate, decay):
    first = BETA_FIRST * moment + (1.0 - BETA_FIRST) * gradient
    second = BETA_SECOND * square + (1.0 - BETA_SECOND) * gradient * gradient
    first_hat = first / (1.0 - BETA_FIRST**STEP)
    second_hat = second / (1.0 - BETA_SECOND**STEP)
    updated = weight - rate * (first_hat / (jnp.sqrt(second_hat) + ADAM_EPS) + decay * weight)
    return (first, second, updated)


def dot(left, right):
    return jnp.dot(left, right, preferred_element_type=FULL)


def dot_last(left, right):
    return lax.dot_general(left, right, (((1,), (1,)), ((), ())), preferred_element_type=FULL)


def dot_first(left, right):
    return lax.dot_general(left, right, (((0,), (0,)), ((), ())), preferred_element_type=FULL)


def block_at(rank, index):
    return lax.rem(index + RING - rank, RING)


def bias_of(pos_row, query_block, key_block, length):
    keys = key_block * length + lax.broadcasted_iota(jnp.int32, (length, length), 0)
    queries = query_block * length + lax.broadcasted_iota(jnp.int32, (length, length), 1)
    allowed = (keys <= queries) & (keys >= queries - pos_row)
    return jnp.where(allowed, 0.0, MASK_FILL)


def head_cols(part, slot):
    first = part * SPAN + slot * HEAD_DIM
    return slice(first, first + HEAD_DIM)


def attend_forward(rank_ref, pos_ref, qkv_ref, heads_ref, lse_ref, turned_ref):
    rank = rank_ref[0]
    length = qkv_ref.shape[1]
    scale = HEAD_DIM ** (-0.5)
    for key_block in range(RING):
        at = block_at(rank, key_block)
        turned_ref[key_block] = qkv_ref[at, :, 2 * SPAN : 3 * SPAN].T
    for query_block in range(RING):
        at = block_at(rank, query_block)
        pos_row = pos_ref[at]
        biases = [bias_of(pos_row, query_block, k, length) for k in range(query_block + 1)]
        columns = []
        for slot in range(SLOTS):
            query = qkv_ref[at, :, head_cols(0, slot)] * jnp.asarray(scale, LOW)
            scores = [
                dot_last(qkv_ref[block_at(rank, k), :, head_cols(1, slot)], query) + biases[k]
                for k in range(query_block + 1)
            ]
            peak = jnp.max(scores[0], axis=0, keepdims=True)
            for part in scores[1:]:
                peak = jnp.maximum(peak, jnp.max(part, axis=0, keepdims=True))
            terms = [jnp.exp(part - peak) for part in scores]
            total = jnp.sum(terms[0], axis=0, keepdims=True)
            for part in terms[1:]:
                total = total + jnp.sum(part, axis=0, keepdims=True)
            inverse = 1.0 / total
            result = None
            for k in range(query_block + 1):
                value = turned_ref[k, slot * HEAD_DIM : (slot + 1) * HEAD_DIM, :]
                term = dot(value, (terms[k] * inverse).astype(LOW))
                result = term if result is None else result + term
            columns.append(result)
            lse_ref[at, slot : slot + 1, :] = peak + jnp.log(total)
        heads_ref[at] = jnp.concatenate(columns, axis=0).T.astype(LOW)


def attend_backward(
    rank_ref, pos_ref, qkv_ref, grad_ref, lse_ref, out_ref, turned_ref, bias_ref
):
    rank = rank_ref[0]
    length = qkv_ref.shape[1]
    scale = HEAD_DIM ** (-0.5)
    pairs = [(q, k) for q in range(RING) for k in range(q + 1)]
    for key_block in range(RING):
        turned_ref[key_block] = qkv_ref[block_at(rank, key_block), :, SPAN : 2 * SPAN].T
    for number, (q, k) in enumerate(pairs):
        bias_ref[number] = bias_of(pos_ref[block_at(rank, q)], q, k, length)
    for slot in range(SLOTS):
        rows = slice(slot * HEAD_DIM, (slot + 1) * HEAD_DIM)
        keys = [qkv_ref[block_at(rank, k), :, head_cols(1, slot)] for k in range(RING)]
        values = [qkv_ref[block_at(rank, k), :, head_cols(2, slot)] for k in range(RING)]
        d_keys = [None] * RING
        d_values = [None] * RING
        if slot == SLOTS - 1:
            keep = jnp.where(rank == RING - 1, 1.0, 0.0)
        else:
            keep = None

        def finish(item):
            return (item if keep is None else item * keep).astype(LOW)

        for q in range(RING):
            at = block_at(rank, q)
            query = qkv_ref[at, :, head_cols(0, slot)] * jnp.asarray(scale, LOW)
            grad = grad_ref[at, :, rows]
            lse = lse_ref[at, slot : slot + 1, :]
            probs = []
            d_probs = []
            inner = None
            for k in range(q + 1):
                score = dot_last(keys[k], query) + bias_ref[pairs.index((q, k))]
                prob = jnp.exp(score - lse)
                d_prob = dot_last(values[k], grad)
                term = jnp.sum(prob * d_prob, axis=0, keepdims=True)
                inner = term if inner is None else inner + term
                probs.append(prob)
                d_probs.append(d_prob)
            d_query = None
            for k in range(q + 1):
                d_score = (probs[k] * (d_probs[k] - inner)).astype(LOW)
                d_key = dot(d_score, query)
                d_value = dot(probs[k].astype(LOW), grad)
                term = dot(turned_ref[k, rows, :], d_score)
                d_keys[k] = d_key if d_keys[k] is None else d_keys[k] + d_key
                d_values[k] = d_value if d_values[k] is None else d_values[k] + d_value
                d_query = term if d_query is None else d_query + term
            out_ref[at, :, head_cols(0, slot)] = finish(d_query.T * scale)
        for k in range(RING):
            at = block_at(rank, k)
            out_ref[at, :, head_cols(1, slot)] = finish(d_keys[k])
            out_ref[at, :, head_cols(2, slot)] = finish(d_values[k])


VMEM_SPEC = pl.BlockSpec(memory_space=pltpu.VMEM)
SMEM_SPEC = pl.BlockSpec(memory_space=pltpu.SMEM)
KERNEL_PARAMS = pltpu.CompilerParams(vmem_limit_bytes=50 * 1024 * 1024)


def lanes_of(width):
    return -(-width // 128) * 128


def store_wide(ref, value):
    width = value.shape[1]
    ref[:, :width] = value.astype(ref.dtype)
    if ref.shape[1] > width:
        ref[:, width:] = jnp.zeros((ref.shape[0], ref.shape[1] - width), ref.dtype)


def shaped(shape, dtype):
    return jax.ShapeDtypeStruct(tuple(shape), dtype)


def call(kernel, outs, ranks, *operands, scratch=(), flops=0, moved=0, first_specs=()):
    return pl.pallas_call(
        kernel,
        grid=(1,) if first_specs else (),
        out_shape=tuple(outs),
        in_specs=[SMEM_SPEC]
        + list(first_specs)
        + [VMEM_SPEC] * (len(operands) - len(first_specs)),
        out_specs=tuple([VMEM_SPEC] * len(outs)),
        scratch_shapes=list(scratch),
        compiler_params=KERNEL_PARAMS,
        cost_estimate=pl.CostEstimate(flops=flops, bytes_accessed=moved, transcendentals=0),
    )(ranks, *operands)


def run_forward(ranks, pos, qkv):
    blocks, length, unused = qkv.shape

    def kernel(ranks_ref, pos_ref, qkv_ref, h0, h1, h2, h3, lse_ref, heads_ref, turned_ref):
        attend_forward(ranks_ref, pos_ref, qkv_ref, heads_ref, lse_ref, turned_ref)
        for index, ref in enumerate((h0, h1, h2, h3)):
            ref[...] = heads_ref[index]

    return call(
        kernel,
        [shaped((length, SPAN), LOW)] * RING + [shaped((blocks, 8, length), FULL)],
        ranks,
        pos,
        qkv,
        scratch=[
            pltpu.VMEM((blocks, length, SPAN), LOW),
            pltpu.VMEM((blocks, SPAN, length), LOW),
        ],
        flops=4_000_000_000,
        moved=16 << 20,
    )


def run_backward(ranks, pos, qkv, grads, lse):
    blocks, length, width = qkv.shape

    def kernel(
        ranks_ref, pos_ref, qkv_ref, g0, g1, g2, g3, lse_ref, out_ref, grad_ref, turned_ref, bias_ref
    ):
        for index, ref in enumerate((g0, g1, g2, g3)):
            grad_ref[index] = ref[...]
        attend_backward(
            ranks_ref, pos_ref, qkv_ref, grad_ref, lse_ref, out_ref, turned_ref, bias_ref
        )

    return call(
        kernel,
        [shaped((blocks, length, width), LOW)],
        ranks,
        pos,
        qkv,
        *grads,
        lse,
        scratch=[
            pltpu.VMEM((blocks, length, SPAN), LOW),
            pltpu.VMEM((blocks, SPAN, length), LOW),
            pltpu.VMEM((10, length, length), FULL),
        ],
        flops=8_000_000_000,
        moved=32 << 20,
    )[0]


def normed(rows):
    centre = rows - jnp.mean(rows, axis=-1, keepdims=True)
    spread = jnp.mean(centre * centre, axis=-1, keepdims=True)
    scale = lax.rsqrt(spread + NORM_EPS)
    return centre * scale, scale


def norm_back(rows, gain, d_rows):
    unit, scale = normed(rows)
    d_unit = d_rows * gain
    mean_one = jnp.mean(d_unit, axis=-1, keepdims=True)
    mean_two = jnp.mean(d_unit * unit, axis=-1, keepdims=True)
    d_inputs = scale * (d_unit - mean_one - unit * mean_two)
    d_gain = jnp.sum(d_rows * unit, axis=0, keepdims=True)
    d_shift = jnp.sum(d_rows, axis=0, keepdims=True)
    return d_inputs, d_gain, d_shift


def spread_rows(refs):
    first = 0
    placed = []
    for ref in refs:
        placed.append((ref, first, ref.shape[0]))
        first += ref.shape[0]
    return placed


def run_enter(ranks, gathered, pieces):
    parts, rows, unused = gathered.shape
    width = parts * rows
    length = pieces[0].shape[0]
    wide = 3 * SPAN
    lanes = 1024

    def kernel(
        ranks_ref, got_ref, small_ref, t0, t1, t2, t3, t4,
        weight_ref, vec_ref, one_ref, qkv_ref, work_ref, bias_ref,
    ):
        for d in range(parts):
            work_ref[d * rows : (d + 1) * rows, :lanes] = got_ref[d].astype(FULL)
            work_ref[d * rows : (d + 1) * rows, lanes:] = small_ref[d].astype(FULL)
        weight_ref[...] = work_ref[:, :wide].astype(LOW)
        vec_ref[...] = work_ref[:, lanes:].T[:16]
        start = pl.multiple_of(ranks_ref[0] * GROUP, GROUP)
        bias_ref[0:1, :SPAN] = vec_ref[2:3, pl.ds(start, SPAN)]
        bias_ref[0:1, SPAN : 2 * SPAN] = jnp.zeros((1, SPAN), FULL)
        bias_ref[0:1, 2 * SPAN :] = vec_ref[3:4, pl.ds(start, SPAN)]
        for ref, first, count in spread_rows((t0, t1, t2, t3, t4)):
            unit, unused = normed(ref[:, :width].astype(FULL))
            low = (unit * vec_ref[0:1, :] + vec_ref[1:2, :]).astype(LOW)
            one_ref[first : first + count, :] = low
            qkv = dot(low, weight_ref[...]) + bias_ref[0:1, :]
            within = first % length
            qkv_ref[first // length, within : within + count, :] = qkv.astype(LOW)

    return call(
        kernel,
        [
            shaped((width, wide), LOW),
            shaped((16, width), FULL),
            shaped((RING * length, width), LOW),
            shaped((RING, length, wide), LOW),
        ],
        ranks,
        gathered,
        gathered,
        *pieces,
        scratch=[pltpu.VMEM((width, lanes + 128), FULL), pltpu.VMEM((8, wide), FULL)],
        first_specs=[
            pl.BlockSpec((parts, rows, lanes), lambda i: (0, 0, 0), memory_space=pltpu.VMEM),
            pl.BlockSpec(
                (parts, rows, 128),
                lambda i: (0, 0, gathered.shape[2] // 128 - 1),
                memory_space=pltpu.VMEM,
            ),
        ],
        flops=2 * RING * length * width * wide,
        moved=16 << 20,
    )


def down_row(d, rows, rows_y):
    z, rest = divmod(d, rows_y * CORES)
    return (rest * RING + z) * rows


def run_unpack(ranks, gathered, column, count, is_down):
    parts, rows, unused = gathered.shape
    width = parts * rows
    rows_y = parts // (RING * CORES)

    def kernel(ranks_ref, got_ref, *refs):
        work_ref = refs[count]
        for index, ref in enumerate(refs[:count]):
            lane = column + index * width
            for d in range(parts):
                first = down_row(d, rows, rows_y) if is_down else d * rows
                work_ref[first : first + rows, :] = got_ref[d, :, lane : lane + width].astype(FULL)
            ref[...] = work_ref[...].astype(LOW)

    return call(
        kernel,
        [shaped((width, width), LOW)] * count,
        ranks,
        gathered,
        scratch=[pltpu.VMEM((width, width), FULL)],
        flops=0,
        moved=(8 << 20) * count,
    )


def run_mix(ranks, heads, out_low, tokens, vec):
    length, width = tokens.shape

    def kernel(
        ranks_ref, h0, h1, h2, h3, out_ref, token_ref, vec_ref, heads_ref, mixed_ref, two_ref
    ):
        for m, ref in enumerate((h0, h1, h2, h3)):
            source = lax.rem(ranks_ref[0] + m, RING)
            start = pl.multiple_of(source * GROUP, GROUP)
            heads_ref[:, pl.ds(start, GROUP)] = ref[:, :GROUP]

            @pl.when(source == RING - 1)
            def last():
                heads_ref[:, RING * GROUP :] = ref[:, GROUP:]

        mixed = token_ref[...].astype(FULL) + (
            dot(heads_ref[...], out_ref[...]) + vec_ref[4:5, :]
        )
        mixed_ref[...] = mixed
        unit, unused = normed(mixed)
        store_wide(two_ref, unit * vec_ref[5:6, :] + vec_ref[6:7, :])

    return call(
        kernel,
        [
            shaped((length, width), LOW),
            shaped((length, width), FULL),
            shaped((length, lanes_of(width)), LOW),
        ],
        ranks,
        *heads,
        out_low,
        tokens,
        vec,
        flops=2 * length * width * width,
        moved=8 << 20,
    )


def run_d_act(ranks, pieces, down_low):
    length, width = pieces[0].shape[0], down_low.shape[1]

    def kernel(ranks_ref, c0, c1, c2, c3, c4, down_ref, cot_ref, act_ref):
        for ref, first, count in spread_rows((c0, c1, c2, c3, c4)):
            rows = ref[:, :width]
            cot_ref[first : first + count, :] = rows
            act_ref[first : first + count, :] = dot_last(rows, down_ref[...])

    return call(
        kernel,
        [shaped((RING * length, width), LOW), shaped((RING * length, width), FULL)],
        ranks,
        *pieces,
        down_low,
        flops=2 * RING * length * width * width,
        moved=12 << 20,
    )


def run_ffn(ranks, pieces, up_low, d_act, vec):
    length, width = pieces[0].shape[0], up_low.shape[0]

    def kernel(
        ranks_ref, a0, a1, a2, a3, a4, up_ref, d_act_ref, vec_ref,
        two_ref, act_ref, d_pre_ref, own_ref, p1, p2, p3, sums_ref,
    ):
        for ref, first, count in spread_rows((a0, a1, a2, a3, a4)):
            two_ref[first : first + count, :] = ref[:, :width]
        bias = vec_ref[pl.ds(7 + ranks_ref[0], 1), :]
        total = None
        for block, out_ref in enumerate((own_ref, p1, p2, p3)):
            rows = slice(block * length, (block + 1) * length)
            value = dot(two_ref[rows, :], up_ref[...]) + bias
            square = value * value
            bent = jnp.tanh(GELU_SCALE * (value + GELU_CUBIC * value * square))
            half = 0.5 * (1.0 + bent)
            act_ref[rows, :] = (value * half).astype(LOW)
            slope = half + (0.5 * GELU_SCALE) * value * (1.0 - bent * bent) * (
                1.0 + (3.0 * GELU_CUBIC) * square
            )
            d_pre = (slope * d_act_ref[rows, :]).astype(LOW)
            d_pre_ref[rows, :] = d_pre
            part = jnp.sum(d_pre.astype(FULL), axis=0, keepdims=True)
            total = part if total is None else total + part
            store_wide(out_ref, dot_last(d_pre, up_ref[...]))
        sums_ref[...] = jnp.broadcast_to(total, sums_ref.shape)

    return call(
        kernel,
        [shaped((RING * length, width), LOW)] * 3
        + [shaped((length, width), FULL)]
        + [shaped((length, lanes_of(width)), LOW)] * 3
        + [shaped((8, width), FULL)],
        ranks,
        *pieces,
        up_low,
        d_act,
        vec,
        flops=4 * RING * length * width * width,
        moved=24 << 20,
    )


def run_back_two(ranks, mixed, terms, cot, out_low, vec):
    length, width = mixed.shape

    def kernel(
        ranks_ref, mixed_ref, own_ref, p1, p2, p3, cot_ref, out_ref, vec_ref,
        d_mixed_ref, branch_ref, d0, d1, d2, d3, sums_ref, work_ref,
    ):
        d_two = own_ref[...] + (
            p1[:, :width].astype(FULL) + p2[:, :width].astype(FULL) + p3[:, :width].astype(FULL)
        )
        d_inputs, d_gain, d_shift = norm_back(mixed_ref[...], vec_ref[5:6, :], d_two)
        cot_rows = cot_ref[...].astype(FULL)
        d_mixed = cot_rows + d_inputs
        d_mixed_ref[...] = d_mixed
        branch = d_mixed.astype(LOW)
        branch_ref[...] = branch
        sums_ref[0:1, :] = d_gain
        sums_ref[1:2, :] = d_shift
        sums_ref[2:3, :] = jnp.sum(branch.astype(FULL), axis=0, keepdims=True)
        sums_ref[3:4, :] = jnp.sum(cot_rows, axis=0, keepdims=True)
        sums_ref[4:8, :] = jnp.zeros((4, width), FULL)
        work_ref[...] = dot_last(branch, out_ref[...]).astype(LOW)
        for r, ref in enumerate((d0, d1, d2, d3)):
            start = pl.multiple_of(lax.rem(ranks_ref[0] + r, RING) * GROUP, GROUP)
            ref[...] = work_ref[:, pl.ds(start, SPAN)]

    return call(
        kernel,
        [shaped((length, width), FULL), shaped((length, width), LOW)]
        + [shaped((length, SPAN), LOW)] * RING
        + [shaped((8, width), FULL)],
        ranks,
        mixed,
        *terms,
        cot,
        out_low,
        vec,
        scratch=[pltpu.VMEM((length, width), LOW)],
        flops=2 * length * width * width,
        moved=10 << 20,
    )


def run_back_one(ranks, tokens, terms, d_mixed, vec):
    length, width = tokens.shape

    def kernel(ranks_ref, token_ref, own_ref, p1, p2, p3, d_mixed_ref, vec_ref, out_ref, sums_ref):
        d_one = own_ref[...] + (
            p1[:, :width].astype(FULL) + p2[:, :width].astype(FULL) + p3[:, :width].astype(FULL)
        )
        d_inputs, d_gain, d_shift = norm_back(
            token_ref[...].astype(FULL), vec_ref[0:1, :], d_one
        )
        out_ref[...] = d_mixed_ref[...] + d_inputs
        sums_ref[0:1, :] = d_gain
        sums_ref[1:2, :] = d_shift
        sums_ref[2:8, :] = jnp.zeros((6, width), FULL)

    return call(
        kernel,
        [shaped((length, width), FULL), shaped((8, width), FULL)],
        ranks,
        tokens,
        *terms,
        d_mixed,
        vec,
        flops=0,
        moved=6 << 20,
    )


def run_project(ranks, left, right, turned):
    length = left.shape[0] // RING
    width = right.shape[0] if turned else right.shape[1]

    def kernel(ranks_ref, left_ref, right_ref, own_ref, p1, p2, p3):
        for block, out_ref in enumerate((own_ref, p1, p2, p3)):
            rows = left_ref[block * length : (block + 1) * length, :]
            product = dot_last(rows, right_ref[...]) if turned else dot(rows, right_ref[...])
            store_wide(out_ref, product)

    return call(
        kernel,
        [shaped((length, width), FULL)] + [shaped((length, lanes_of(width)), LOW)] * 3,
        ranks,
        left,
        right,
        flops=2 * left.shape[0] * left.shape[1] * width,
        moved=8 << 20,
    )


def run_grads(ranks, two, d_pre, act, cot, rows, rows_y):
    width = two.shape[1]
    parts = width // rows
    padded = -(-rows // 8) * 8
    strip = width // RING

    def kernel(ranks_ref, two_ref, d_pre_ref, act_ref, cot_ref, out_ref, turned_ref, work_ref):
        out_ref[:, rows:, :] = jnp.zeros((parts, padded - rows, 2 * width), FULL)
        for index, (left, right) in enumerate(((two_ref, d_pre_ref), (act_ref, cot_ref))):
            turned_ref[...] = left[...].T
            for block in range(RING):
                part = slice(block * strip, (block + 1) * strip)
                work_ref[part, :] = dot(turned_ref[part, :], right[...])
            for d in range(parts):
                first = down_row(d, rows, rows_y) if index else d * rows
                out_ref[d, :rows, index * width : (index + 1) * width] = work_ref[
                    first : first + rows, :
                ]

    return call(
        kernel,
        [shaped((parts, padded, 2 * width), FULL)],
        ranks,
        two,
        d_pre,
        act,
        cot,
        scratch=[pltpu.VMEM((width, two.shape[0]), LOW), pltpu.VMEM((width, width), FULL)],
        flops=4 * two.shape[0] * width * width,
        moved=32 << 20,
    )[0]


def padded_rows(rows):
    return -(-rows // 8) * 8


def fill_by_core(ranks_ref, work_ref, keep_ref, send_ref, rows):
    parts = work_ref.shape[0] // rows
    for ref in (keep_ref, send_ref):
        ref[:, rows:, :] = jnp.zeros((ref.shape[0], ref.shape[1] - rows, ref.shape[2]), LOW)

    def fill(own_core):
        for d in range(parts):
            ref = keep_ref if d % CORES == own_core else send_ref
            ref[d // CORES, :rows, :] = work_ref[d * rows : (d + 1) * rows, :].astype(LOW)

    @pl.when(ranks_ref[1] == 0)
    def even():
        fill(0)

    @pl.when(ranks_ref[1] == 1)
    def odd():
        fill(1)


def run_grad_out(ranks, heads, pieces, rows):
    width = heads.shape[1]
    size = pieces[0].shape[1]
    lanes = lanes_of(size)
    half = width // rows // CORES

    def kernel(ranks_ref, heads_ref, b0, b1, b2, b3, keep_ref, send_ref, work_ref):
        turned = heads_ref[...].T
        for index, ref in enumerate((b0, b1, b2, b3)):
            first = index * lanes
            work_ref[:, first : first + size] = dot(turned, ref[...])
            work_ref[:, first + size : first + lanes] = jnp.zeros((width, lanes - size), FULL)
        fill_by_core(ranks_ref, work_ref, keep_ref, send_ref, rows)

    return call(
        kernel,
        [shaped((half, padded_rows(rows), RING * lanes), LOW)] * 2,
        ranks,
        heads,
        *pieces,
        scratch=[pltpu.VMEM((width, RING * lanes), FULL)],
        flops=2 * heads.shape[0] * width * width,
        moved=8 << 20,
    )


def run_out_blocks(ranks, keep, came, size):
    half, padded, wide = keep.shape
    lanes = wide // RING
    total = half * padded

    def kernel(ranks_ref, keep_ref, came_ref, *refs):
        for index, ref in enumerate(refs):
            part = slice(index * lanes, (index + 1) * lanes)
            rows = keep_ref[:, :, part].astype(FULL) + came_ref[:, :, part].astype(FULL)
            store_wide(ref, rows.reshape(total, lanes).T[:size])

    return call(
        kernel,
        [shaped((size, lanes_of(total)), FULL)] + [shaped((size, lanes_of(total)), LOW)] * 3,
        ranks,
        keep,
        came,
        flops=0,
        moved=6 << 20,
    )


def run_pack(ranks, one, d_qkv, rows):
    width = one.shape[1]
    wide = d_qkv.shape[1]
    lanes = lanes_of(wide)
    half = width // rows // CORES
    strip = width // RING

    def kernel(ranks_ref, one_ref, grad_ref, keep_ref, send_ref, turned_ref, work_ref):
        turned_ref[...] = one_ref[...].T
        for block in range(RING):
            part = slice(block * strip, (block + 1) * strip)
            work_ref[part, :wide] = dot(turned_ref[part, :], grad_ref[...])
        work_ref[:, wide:] = jnp.zeros((width, lanes - wide), FULL)
        fill_by_core(ranks_ref, work_ref, keep_ref, send_ref, rows)

    return call(
        kernel,
        [shaped((half, padded_rows(rows), lanes), LOW)] * 2,
        ranks,
        one,
        d_qkv,
        scratch=[pltpu.VMEM((width, one.shape[0]), LOW), pltpu.VMEM((width, lanes), FULL)],
        flops=2 * one.shape[0] * width * wide,
        moved=12 << 20,
    )


def run_join(ranks, keep, came, outs, wide, rows, rows_y):
    half, padded, unused = keep.shape
    size = outs[0].shape[0]
    total = half * padded
    lanes = lanes_of(wide + size)

    def kernel(ranks_ref, keep_ref, came_ref, o0, o1, o2, o3, *refs):
        work_ref = refs[rows_y]
        work_ref[:, :, :wide] = keep_ref[:, :, :wide].astype(FULL) + came_ref[
            :, :, :wide
        ].astype(FULL)
        out_sum = (o0[:, :total].astype(FULL) + o1[:, :total].astype(FULL)) + (
            o2[:, :total].astype(FULL) + o3[:, :total].astype(FULL)
        )
        work_ref[:, :, wide : wide + size] = out_sum.T.reshape(half, padded, size)
        work_ref[:, :, wide + size :] = jnp.zeros((half, padded, lanes - wide - size), FULL)
        for r, ref in enumerate(refs[:rows_y]):
            at = lax.rem(ranks_ref[2] + r, rows_y)
            for z in range(RING):
                ref[z] = work_ref[z * rows_y + at, :rows, :].astype(ref.dtype)

    return call(
        kernel,
        [shaped((RING, rows, lanes), FULL)] + [shaped((RING, rows, lanes), LOW)] * (rows_y - 1),
        ranks,
        keep,
        came,
        *outs,
        scratch=[pltpu.VMEM((half, padded, lanes), FULL)],
        flops=0,
        moved=8 << 20,
    )


def run_fold_z(ranks, terms, rows):
    groups, unused, width = terms[0].shape

    def kernel(ranks_ref, *refs):
        ins, outs = refs[: len(terms)], refs[len(terms) :]
        for r, out_ref in enumerate(outs):
            at = lax.rem(ranks_ref[3] + r, RING)
            total = ins[0][at].astype(FULL)
            for ref in ins[1:]:
                total = total + ref[at].astype(FULL)
            out_ref[...] = total.astype(out_ref.dtype)

    return call(
        kernel,
        [shaped((rows, width), FULL)] + [shaped((rows, width), LOW)] * 3,
        ranks,
        *terms,
        flops=0,
        moved=4 << 20,
    )


def run_down(ranks, act, down):
    width = down.shape[1]
    length = act.shape[0] // RING

    def kernel(ranks_ref, act_ref, down_ref, out_ref):
        for block in range(RING):
            at = lax.rem(ranks_ref[0] + block, RING)
            product = dot(act_ref[block * length : (block + 1) * length, :], down_ref[...])
            out_ref[at, :, :width] = product.astype(LOW)
            out_ref[at, :, width:] = jnp.zeros((length, lanes_of(width) - width), LOW)

    return call(
        kernel,
        [shaped((RING, length, lanes_of(width)), LOW)],
        ranks,
        act,
        down,
        flops=2 * act.shape[0] * act.shape[1] * width,
        moved=8 << 20,
    )[0]


def after(item, *others):
    return lax.optimization_barrier((item,) + others)[0]


def permute(item, axes, pairs):
    return lax.ppermute(item, axes, pairs)


def ctx_shift(item, step):
    return permute(item, "ctx", [(i, (i + step) % RING) for i in range(RING)])


def gather_pieces(item, *between):
    half = item.shape[0] // 2
    left = ctx_shift(item, 1)
    right = ctx_shift(item, 3)
    left, right = lax.optimization_barrier((left, right) + between)[:2]
    top = ctx_shift(left[:half], 1)
    bottom = ctx_shift(right[half:], 3)
    return (item, right, top, bottom, left)


def gather_small(item):
    return jnp.stack([item, ctx_shift(item, 3), ctx_shift(item, 2), ctx_shift(item, 1)])


def to_global(relative, rank):
    doubled = jnp.concatenate([relative, relative[: RING - 1]], axis=0)
    return lax.dynamic_slice_in_dim(doubled, lax.rem(RING - rank, RING), RING, axis=0)


def exchange(pieces):
    return [pieces[0]] + [ctx_shift(pieces[RING - r], RING - r) for r in (1, 2, 3)]


def send_on(pieces):
    return [pieces[0]] + [ctx_shift(pieces[r], r) for r in (1, 2, 3)]


def dp_perm(dp_count, move):
    rows = dp_count // (RING * CORES)
    pairs = []
    for z in range(RING):
        for y in range(rows):
            for core in range(CORES):
                to_z, to_y, to_core = move(z, y, core, rows)
                pairs.append(((z * rows + y) * CORES + core, (to_z * rows + to_y) * CORES + to_core))
    return pairs


def swap_core(item, dp_count):
    return permute(
        item, "dp", dp_perm(dp_count, lambda z, y, core, rows: (z, y, 1 - core))
    )


def send_axis(pieces, axis, dp_count):
    came = [pieces[0]]
    for step, piece in enumerate(pieces[1:], 1):
        if axis == "z":
            perm = dp_perm(dp_count, lambda z, y, core, rows: ((z + step) % RING, y, core))
        else:
            perm = dp_perm(dp_count, lambda z, y, core, rows: (z, (y + step) % rows, core))
        came.append(permute(piece, "dp", perm))
    return came


def sum_everywhere(item, dp_count, beside):
    rows = dp_count // (RING * CORES)
    item = item + swap_core(item, dp_count)
    for name in ("y", "z", "x"):
        if name == "x":
            item, *beside = lax.optimization_barrier((item,) + tuple(beside))
        parts = [item]
        for step in (1, 2, 3):
            if name == "x":
                perm = [(i, i ^ step) for i in range(RING)]
                parts.append(lax.ppermute(item, "ctx", perm))
            elif name == "z":
                perm = dp_perm(dp_count, lambda z, y, core, rows: (z ^ step, y, core))
                parts.append(lax.ppermute(item, "dp", perm))
            elif rows == RING:
                perm = dp_perm(dp_count, lambda z, y, core, rows: (z, y ^ step, core))
                parts.append(lax.ppermute(item, "dp", perm))
        if len(parts) == RING:
            item = (parts[0] + parts[1]) + (parts[2] + parts[3])
    return item, *beside


def plane_pairs(dp_count, step):
    inner = dp_count // RING
    return [
        ((z * inner + rest) * RING + x, (((x + step) % RING) * inner + rest) * RING + z)
        for z in range(RING)
        for rest in range(inner)
        for x in range(RING)
    ]


def body(
    tokens,
    cotangent,
    positions,
    w_qkv,
    w_out,
    w_up,
    w_down,
    vectors,
    moment_qkv,
    square_qkv,
    moment_out,
    square_out,
    moment_up,
    square_up,
    moment_down,
    square_down,
    moment_vec,
    square_vec,
):
    unused, local_len, width = tokens.shape
    dp_count = lax.axis_size("dp")
    rows_y = dp_count // (RING * CORES)
    rank = lax.axis_index("ctx")
    dp_rank = lax.axis_index("dp")
    rank_core = lax.rem(dp_rank, CORES)
    rank_y = lax.rem(lax.div(dp_rank, CORES), rows_y)
    rank_z = lax.div(dp_rank, CORES * rows_y)
    ranks = jnp.stack([rank, rank_core, rank_y, rank_z]).astype(jnp.int32)
    row_size = w_qkv.shape[0]
    full_len = local_len * RING

    shard_cols = jnp.concatenate(
        [w_qkv.astype(LOW), w_out.astype(LOW), vectors.astype(LOW)], axis=1
    )
    gathered = to_global(gather_small(shard_cols), rank)
    qkv_size, out_size = w_qkv.shape[1], w_out.shape[1]
    qkv_rows = jnp.concatenate([gathered[s, :, :qkv_size] for s in range(RING)], axis=1)
    out_rows = jnp.concatenate(
        [gathered[s, :, qkv_size : qkv_size + out_size] for s in range(RING)], axis=1
    )
    vec_rows = jnp.concatenate([gathered[s, :, qkv_size + out_size :] for s in range(RING)], axis=1)
    head_start = rank * GROUP
    qkv_own = [
        lax.dynamic_slice_in_dim(qkv_rows[:, part * width : (part + 1) * width], head_start, SPAN, 1)
        for part in range(3)
    ]
    ahead = 3 * SPAN + 2 * width
    vec_wide = jnp.pad(
        vec_rows, ((0, 0), (lanes_of(ahead) - ahead, 128 - vec_rows.shape[1]))
    )
    weights_all = lax.all_gather(
        jnp.concatenate(qkv_own + [out_rows, w_up.astype(LOW), vec_wide], axis=1),
        "dp",
        axis=0,
        tiled=False,
    )
    token_low = tokens.reshape(local_len, width)
    cot_low = cotangent.reshape(local_len, width)
    lane_fill = ((0, 0), (0, lanes_of(width) - width))
    token_pieces = gather_pieces(jnp.pad(token_low, lane_fill))
    pos_seq = gather_small(after(positions, *token_pieces))

    down_low_shard = after(w_down.astype(LOW), *token_pieces)
    down_parts = []
    for step in range(RING):
        quarter = lax.dynamic_slice_in_dim(
            down_low_shard, lax.rem(rank + step, RING) * row_size, row_size, 0
        )
        down_parts.append(permute(quarter, ("dp", "ctx"), plane_pairs(dp_count, step)))
    down_turned = jnp.stack([down_parts[(RING - m) % RING] for m in range(RING)])
    down_cols = to_global(down_turned, rank_z)
    down_all = lax.all_gather(
        jnp.concatenate([down_cols[s] for s in range(RING)], axis=1), "dp", axis=0, tiled=False
    )

    qkv_low, vec, a_one, qkv_blocks = run_enter(
        ranks, after(weights_all, pos_seq), token_pieces
    )
    cot_pieces = gather_pieces(
        after(jnp.pad(cot_low, lane_fill), down_cols, pos_seq), qkv_blocks
    )
    *heads_pieces, lse = run_forward(ranks, pos_seq, qkv_blocks)
    out_low, up_low = run_unpack(ranks, weights_all, 3 * SPAN, 2, False)
    (down_low,) = run_unpack(ranks, down_all, 0, 1, True)
    heads_came = exchange(heads_pieces)
    heads_low, mixed, a_two = run_mix(
        ranks, heads_came, after(out_low, *cot_pieces), token_low, vec
    )
    cot_seq, d_act = run_d_act(ranks, cot_pieces, down_low)
    two_pieces = gather_pieces(a_two, d_act)
    a_two_seq, act_low, d_pre, own_two, p1, p2, p3, d_pre_sums = run_ffn(
        ranks, two_pieces, up_low, d_act, vec
    )
    d_two_terms = send_on([own_two, p1, p2, p3])

    grads_two = run_grads(ranks, a_two_seq, d_pre, act_low, cot_seq, row_size, rows_y)
    down_rows = run_down(ranks, act_low, down_low)
    gate = lax.optimization_barrier(tuple(d_two_terms) + (grads_two, down_rows))
    d_two_terms = gate[:4]
    grads_two, down_rows = gate[4:]
    summed_two = lax.psum_scatter(
        grads_two.reshape(dp_count * grads_two.shape[1], 2 * width),
        "dp",
        scatter_dimension=0,
        tiled=True,
    )
    summed_two, down_rows = lax.optimization_barrier((summed_two, down_rows))
    down_sum = lax.psum_scatter(
        down_rows.reshape(full_len, down_rows.shape[2]), "ctx", scatter_dimension=0, tiled=True
    )
    down_sum = lax.optimization_barrier(down_sum)[:, :width].astype(FULL)
    grad_up = summed_two[:row_size, :width]
    grad_down_rows = summed_two[:row_size, width:]

    d_mixed, d_branch, g0, g1, g2, g3, sums_two = run_back_two(
        ranks, mixed, d_two_terms, cot_low, out_low, vec
    )
    d_heads_came = exchange([g0, g1, g2, g3])
    out_keep, out_send = run_grad_out(
        ranks,
        heads_low,
        [
            lax.dynamic_slice_in_dim(d_branch, lax.rem(rank + r, RING) * out_size, out_size, 1)
            for r in range(RING)
        ],
        row_size,
    )
    out_blocks = run_out_blocks(ranks, out_keep, swap_core(out_send, dp_count), out_size)
    gate = lax.optimization_barrier(tuple(d_heads_came) + tuple(out_blocks))
    d_heads_came = gate[:4]
    out_came = send_on(gate[4:])
    d_qkv_blocks = run_backward(ranks, pos_seq, qkv_blocks, d_heads_came, lse)
    gate = lax.optimization_barrier((d_qkv_blocks,) + tuple(out_came))
    d_qkv = gate[0].reshape(full_len, 3 * SPAN)
    out_came = gate[1:]
    qkv_keep, qkv_send = run_pack(ranks, a_one, d_qkv, row_size)
    qkv_came = swap_core(qkv_send, dp_count)
    one_pieces = run_project(ranks, after(d_qkv, qkv_keep), qkv_low, True)
    d_one_terms = send_on(one_pieces)
    qkv_came = after(qkv_came, *one_pieces)
    parts = run_join(ranks, qkv_keep, qkv_came, out_came, 3 * SPAN, row_size, rows_y)
    gate = lax.optimization_barrier(tuple(send_axis(parts, "y", dp_count)) + tuple(d_one_terms))
    parts = run_fold_z(ranks, gate[:rows_y], row_size)
    d_one_terms = gate[rows_y:]
    d_token_rows, sums_one = run_back_one(ranks, token_low, d_one_terms, d_mixed, vec)
    d_tokens = d_token_rows.reshape(tokens.shape)
    came = send_axis(parts, "z", dp_count)
    grad_last = came[0] + (came[1].astype(FULL) + came[2].astype(FULL) + came[3].astype(FULL))
    grad_qkv_own = grad_last[:, : 3 * SPAN]
    grad_out = grad_last[:, 3 * SPAN : 3 * SPAN + out_size]

    down_quarters = []
    for step in range(RING):
        block = lax.dynamic_slice_in_dim(
            grad_down_rows, lax.rem(rank_z + RING - step, RING) * out_size, out_size, 1
        )
        back = [(target, source) for source, target in plane_pairs(dp_count, step)]
        down_quarters.append(permute(block, ("dp", "ctx"), back))
    grad_down = to_global(jnp.stack(down_quarters), rank).reshape(RING * row_size, out_size)

    d_qkv_sums = jnp.sum(d_qkv.astype(FULL), axis=0)
    empty = jnp.zeros((width,), FULL)
    vec_terms = jnp.stack(
        [
            sums_one[0],
            sums_one[1],
            lax.dynamic_update_slice(empty, d_qkv_sums[:SPAN], (head_start,)),
            lax.dynamic_update_slice(empty, d_qkv_sums[2 * SPAN :], (head_start,)),
            sums_two[2],
            sums_two[0],
            sums_two[1],
        ]
        + [jnp.where(rank == c, d_pre_sums[0], 0.0) for c in range(RING)]
        + [sums_two[3]],
        axis=0,
    )
    local_sq = (
        jnp.sum(grad_qkv_own * grad_qkv_own)
        + jnp.sum(grad_out * grad_out)
        + jnp.sum(grad_up * grad_up)
        + jnp.sum(grad_down_rows * grad_down_rows)
    )
    vec_count = vec_terms.shape[0]
    first_lane = lax.broadcasted_iota(jnp.int32, (4, width), 1) == 0
    first_row = lax.broadcasted_iota(jnp.int32, (4, width), 0) == 0
    payload = jnp.concatenate(
        [vec_terms, jnp.where(first_lane & first_row, local_sq, 0.0)], axis=0
    )
    qkv_near = gather_small(grad_qkv_own)
    payload, qkv_near, grad_down, down_sum = sum_everywhere(
        payload, dp_count, (qkv_near, grad_down, down_sum)
    )
    vec_total = payload[:vec_count]
    outputs = (mixed + (down_sum + vec[11])).astype(LOW).reshape(tokens.shape)
    total_sq = payload[vec_count, 0] + jnp.sum(vec_total * vec_total)
    grad_norm = jnp.sqrt(total_sq)
    clip_factor = CLIP_LIMIT / jnp.maximum(grad_norm, CLIP_LIMIT)

    col_size = vec_count // RING
    grad_vec = lax.dynamic_slice(
        vec_total, (rank * col_size, dp_rank * row_size), (col_size, row_size)
    ).T
    qkv_groups = to_global(qkv_near, rank)
    grad_qkv_rows = jnp.concatenate(
        [
            qkv_groups[s, :, part * SPAN : part * SPAN + (SPAN if s == RING - 1 else GROUP)]
            for part in range(3)
            for s in range(RING)
        ],
        axis=1,
    )
    grad_qkv = lax.dynamic_slice_in_dim(grad_qkv_rows, rank * qkv_size, qkv_size, 1)

    first_qkv, second_qkv, updated_qkv = adam_step(
        w_qkv, moment_qkv, square_qkv, grad_qkv * clip_factor, LEARN_RATES[0], WEIGHT_DECAYS[0]
    )
    first_out, second_out, updated_out = adam_step(
        w_out, moment_out, square_out, grad_out * clip_factor, LEARN_RATES[1], WEIGHT_DECAYS[1]
    )
    first_up, second_up, updated_up = adam_step(
        w_up, moment_up, square_up, grad_up * clip_factor, LEARN_RATES[2], WEIGHT_DECAYS[2]
    )
    first_down, second_down, updated_down = adam_step(
        w_down, moment_down, square_down, grad_down * clip_factor, LEARN_RATES[3], WEIGHT_DECAYS[3]
    )
    first_vec, second_vec, updated_vec = adam_step(
        vectors, moment_vec, square_vec, grad_vec * clip_factor, LEARN_RATES[4], WEIGHT_DECAYS[4]
    )
    return (
        outputs,
        d_tokens,
        grad_norm,
        first_qkv,
        second_qkv,
        updated_qkv,
        first_out,
        second_out,
        updated_out,
        first_up,
        second_up,
        updated_up,
        first_down,
        second_down,
        updated_down,
        first_vec,
        second_vec,
        updated_vec,
    )


def solution(mesh):
    token_spec = P("dp", "ctx", None)
    flat_spec = P("dp", "ctx")
    return jax.shard_map(
        body,
        mesh=mesh,
        in_specs=(token_spec, token_spec) + (flat_spec,) * 16,
        out_specs=(token_spec, token_spec, P()) + (flat_spec,) * 15,
        check_vma=False,
    )
```

```python
import jax
import jax.numpy as jnp
from jax import lax
from jax.experimental import pallas as pl
from jax.experimental.pallas import tpu as pltpu
from jax.sharding import PartitionSpec as P

HEADS = 17
HEAD_DIM = 64
SLOTS = 5
GROUP = 4 * HEAD_DIM
SPAN = SLOTS * HEAD_DIM
STEP = 10

NORM_EPS = 1e-05
ADAM_EPS = 1e-08
BETA_FIRST = 0.9
BETA_SECOND = 0.999
CLIP_LIMIT = 1.0
GELU_SCALE = 0.7978845608
GELU_CUBIC = 0.044715
MASK_FILL = -1e30
LEARN_RATES = (0.05, 0.5, 0.1, 0.03, 1.0)
WEIGHT_DECAYS = (0.1, 0.1, 0.1, 0.1, 0.0)

LOW = jnp.bfloat16
FULL = jnp.float32
RING = 4
CORES = 2


def layer_norm(inputs, gain_col, shift_col):
    centre = inputs - jnp.mean(inputs, axis=-1, keepdims=True)
    spread = jnp.mean(centre * centre, axis=-1, keepdims=True)
    return centre * lax.rsqrt(spread + NORM_EPS) * gain_col + shift_col


def gelu(inputs):
    inner = GELU_SCALE * (inputs + GELU_CUBIC * inputs * inputs * inputs)
    return 0.5 * inputs * (1.0 + jnp.tanh(inner))


def adam_step(weight, moment, square, gradient, rate, decay):
    first = BETA_FIRST * moment + (1.0 - BETA_FIRST) * gradient
    second = BETA_SECOND * square + (1.0 - BETA_SECOND) * gradient * gradient
    first_hat = first / (1.0 - BETA_FIRST**STEP)
    second_hat = second / (1.0 - BETA_SECOND**STEP)
    updated = weight - rate * (first_hat / (jnp.sqrt(second_hat) + ADAM_EPS) + decay * weight)
    return (first, second, updated)


def dot(left, right):
    return jnp.dot(left, right, preferred_element_type=FULL)


def dot_last(left, right):
    return lax.dot_general(left, right, (((1,), (1,)), ((), ())), preferred_element_type=FULL)


def dot_first(left, right):
    return lax.dot_general(left, right, (((0,), (0,)), ((), ())), preferred_element_type=FULL)


def block_at(rank, index):
    return lax.rem(index + RING - rank, RING)


def bias_of(pos_row, query_block, key_block, length):
    keys = key_block * length + lax.broadcasted_iota(jnp.int32, (length, length), 0)
    queries = query_block * length + lax.broadcasted_iota(jnp.int32, (length, length), 1)
    allowed = (keys <= queries) & (keys >= queries - pos_row)
    return jnp.where(allowed, 0.0, MASK_FILL)


def head_cols(part, slot):
    first = part * SPAN + slot * HEAD_DIM
    return slice(first, first + HEAD_DIM)


def attend_forward(rank_ref, pos_ref, qkv_ref, heads_ref, lse_ref, turned_ref):
    rank = rank_ref[0]
    length = qkv_ref.shape[1]
    scale = HEAD_DIM ** (-0.5)
    for key_block in range(RING):
        at = block_at(rank, key_block)
        turned_ref[key_block] = qkv_ref[at, :, 2 * SPAN : 3 * SPAN].T
    for query_block in range(RING):
        at = block_at(rank, query_block)
        pos_row = pos_ref[at]
        biases = [bias_of(pos_row, query_block, k, length) for k in range(query_block + 1)]
        columns = []
        for slot in range(SLOTS):
            query = qkv_ref[at, :, head_cols(0, slot)] * jnp.asarray(scale, LOW)
            scores = [
                dot_last(qkv_ref[block_at(rank, k), :, head_cols(1, slot)], query) + biases[k]
                for k in range(query_block + 1)
            ]
            peak = jnp.max(scores[0], axis=0, keepdims=True)
            for part in scores[1:]:
                peak = jnp.maximum(peak, jnp.max(part, axis=0, keepdims=True))
            terms = [jnp.exp(part - peak) for part in scores]
            total = jnp.sum(terms[0], axis=0, keepdims=True)
            for part in terms[1:]:
                total = total + jnp.sum(part, axis=0, keepdims=True)
            inverse = 1.0 / total
            result = None
            for k in range(query_block + 1):
                value = turned_ref[k, slot * HEAD_DIM : (slot + 1) * HEAD_DIM, :]
                term = dot(value, (terms[k] * inverse).astype(LOW))
                result = term if result is None else result + term
            columns.append(result)
            lse_ref[at, slot : slot + 1, :] = peak + jnp.log(total)
        heads_ref[at] = jnp.concatenate(columns, axis=0).T.astype(LOW)


def attend_backward(
    rank_ref, pos_ref, qkv_ref, grad_ref, lse_ref, out_ref, turned_ref, bias_ref
):
    rank = rank_ref[0]
    length = qkv_ref.shape[1]
    scale = HEAD_DIM ** (-0.5)
    pairs = [(q, k) for q in range(RING) for k in range(q + 1)]
    for key_block in range(RING):
        turned_ref[key_block] = qkv_ref[block_at(rank, key_block), :, SPAN : 2 * SPAN].T
    for number, (q, k) in enumerate(pairs):
        bias_ref[number] = bias_of(pos_ref[block_at(rank, q)], q, k, length)
    for slot in range(SLOTS):
        rows = slice(slot * HEAD_DIM, (slot + 1) * HEAD_DIM)
        keys = [qkv_ref[block_at(rank, k), :, head_cols(1, slot)] for k in range(RING)]
        values = [qkv_ref[block_at(rank, k), :, head_cols(2, slot)] for k in range(RING)]
        d_keys = [None] * RING
        d_values = [None] * RING
        if slot == SLOTS - 1:
            keep = jnp.where(rank == RING - 1, 1.0, 0.0)
        else:
            keep = None

        def finish(item):
            return (item if keep is None else item * keep).astype(LOW)

        for q in range(RING):
            at = block_at(rank, q)
            query = qkv_ref[at, :, head_cols(0, slot)] * jnp.asarray(scale, LOW)
            grad = grad_ref[at, :, rows]
            lse = lse_ref[at, slot : slot + 1, :]
            probs = []
            d_probs = []
            inner = None
            for k in range(q + 1):
                score = dot_last(keys[k], query) + bias_ref[pairs.index((q, k))]
                prob = jnp.exp(score - lse)
                d_prob = dot_last(values[k], grad)
                term = jnp.sum(prob * d_prob, axis=0, keepdims=True)
                inner = term if inner is None else inner + term
                probs.append(prob)
                d_probs.append(d_prob)
            d_query = None
            for k in range(q + 1):
                d_score = (probs[k] * (d_probs[k] - inner)).astype(LOW)
                d_key = dot(d_score, query)
                d_value = dot(probs[k].astype(LOW), grad)
                term = dot(turned_ref[k, rows, :], d_score)
                d_keys[k] = d_key if d_keys[k] is None else d_keys[k] + d_key
                d_values[k] = d_value if d_values[k] is None else d_values[k] + d_value
                d_query = term if d_query is None else d_query + term
            out_ref[at, :, head_cols(0, slot)] = finish(d_query.T * scale)
        for k in range(RING):
            at = block_at(rank, k)
            out_ref[at, :, head_cols(1, slot)] = finish(d_keys[k])
            out_ref[at, :, head_cols(2, slot)] = finish(d_values[k])


VMEM_SPEC = pl.BlockSpec(memory_space=pltpu.VMEM)
SMEM_SPEC = pl.BlockSpec(memory_space=pltpu.SMEM)
KERNEL_PARAMS = pltpu.CompilerParams(vmem_limit_bytes=50 * 1024 * 1024)


def lanes_of(width):
    return -(-width // 128) * 128


def store_wide(ref, value):
    width = value.shape[1]
    ref[:, :width] = value.astype(ref.dtype)
    if ref.shape[1] > width:
        ref[:, width:] = jnp.zeros((ref.shape[0], ref.shape[1] - width), ref.dtype)


def shaped(shape, dtype):
    return jax.ShapeDtypeStruct(tuple(shape), dtype)


def call(kernel, outs, ranks, *operands, scratch=(), flops=0, moved=0, first_specs=()):
    return pl.pallas_call(
        kernel,
        grid=(1,) if first_specs else (),
        out_shape=tuple(outs),
        in_specs=[SMEM_SPEC]
        + list(first_specs)
        + [VMEM_SPEC] * (len(operands) - len(first_specs)),
        out_specs=tuple([VMEM_SPEC] * len(outs)),
        scratch_shapes=list(scratch),
        compiler_params=KERNEL_PARAMS,
        cost_estimate=pl.CostEstimate(flops=flops, bytes_accessed=moved, transcendentals=0),
    )(ranks, *operands)


def run_forward(ranks, pos, qkv):
    blocks, length, unused = qkv.shape

    def kernel(ranks_ref, pos_ref, qkv_ref, h0, h1, h2, h3, lse_ref, heads_ref, turned_ref):
        attend_forward(ranks_ref, pos_ref, qkv_ref, heads_ref, lse_ref, turned_ref)
        for index, ref in enumerate((h0, h1, h2, h3)):
            ref[...] = heads_ref[index]

    return call(
        kernel,
        [shaped((length, SPAN), LOW)] * RING + [shaped((blocks, 8, length), FULL)],
        ranks,
        pos,
        qkv,
        scratch=[
            pltpu.VMEM((blocks, length, SPAN), LOW),
            pltpu.VMEM((blocks, SPAN, length), LOW),
        ],
        flops=4_000_000_000,
        moved=16 << 20,
    )


def run_backward(ranks, pos, qkv, grads, lse):
    blocks, length, width = qkv.shape

    def kernel(
        ranks_ref, pos_ref, qkv_ref, g0, g1, g2, g3, lse_ref, out_ref, grad_ref, turned_ref, bias_ref
    ):
        for index, ref in enumerate((g0, g1, g2, g3)):
            grad_ref[index] = ref[...]
        attend_backward(
            ranks_ref, pos_ref, qkv_ref, grad_ref, lse_ref, out_ref, turned_ref, bias_ref
        )

    return call(
        kernel,
        [shaped((blocks, length, width), LOW)],
        ranks,
        pos,
        qkv,
        *grads,
        lse,
        scratch=[
            pltpu.VMEM((blocks, length, SPAN), LOW),
            pltpu.VMEM((blocks, SPAN, length), LOW),
            pltpu.VMEM((10, length, length), FULL),
        ],
        flops=8_000_000_000,
        moved=32 << 20,
    )[0]


def normed(rows):
    centre = rows - jnp.mean(rows, axis=-1, keepdims=True)
    spread = jnp.mean(centre * centre, axis=-1, keepdims=True)
    scale = lax.rsqrt(spread + NORM_EPS)
    return centre * scale, scale


def norm_back(rows, gain, d_rows):
    unit, scale = normed(rows)
    d_unit = d_rows * gain
    mean_one = jnp.mean(d_unit, axis=-1, keepdims=True)
    mean_two = jnp.mean(d_unit * unit, axis=-1, keepdims=True)
    d_inputs = scale * (d_unit - mean_one - unit * mean_two)
    d_gain = jnp.sum(d_rows * unit, axis=0, keepdims=True)
    d_shift = jnp.sum(d_rows, axis=0, keepdims=True)
    return d_inputs, d_gain, d_shift


def spread_rows(refs):
    first = 0
    placed = []
    for ref in refs:
        placed.append((ref, first, ref.shape[0]))
        first += ref.shape[0]
    return placed


def run_enter(ranks, gathered, pieces):
    parts, rows, unused = gathered.shape
    width = parts * rows
    length = pieces[0].shape[0]
    wide = 3 * SPAN
    lanes = 1024

    def kernel(
        ranks_ref, got_ref, t0, t1, t2, t3, t4,
        weight_ref, vec_ref, one_ref, qkv_ref, work_ref, bias_ref,
    ):
        for d in range(parts):
            work_ref[d * rows : (d + 1) * rows, :] = got_ref[d].astype(FULL)
        weight_ref[...] = work_ref[:, :wide].astype(LOW)
        vec_ref[...] = work_ref[:, lanes - 128 :].T[wide - lanes + 128 : wide - lanes + 144]
        start = pl.multiple_of(ranks_ref[0] * GROUP, GROUP)
        bias_ref[0:1, :SPAN] = vec_ref[2:3, pl.ds(start, SPAN)]
        bias_ref[0:1, SPAN : 2 * SPAN] = jnp.zeros((1, SPAN), FULL)
        bias_ref[0:1, 2 * SPAN :] = vec_ref[3:4, pl.ds(start, SPAN)]
        for ref, first, count in spread_rows((t0, t1, t2, t3, t4)):
            unit, unused = normed(ref[:, :width].astype(FULL))
            low = (unit * vec_ref[0:1, :] + vec_ref[1:2, :]).astype(LOW)
            one_ref[first : first + count, :] = low
            qkv = dot(low, weight_ref[...]) + bias_ref[0:1, :]
            within = first % length
            qkv_ref[first // length, within : within + count, :] = qkv.astype(LOW)

    return call(
        kernel,
        [
            shaped((width, wide), LOW),
            shaped((16, width), FULL),
            shaped((RING * length, width), LOW),
            shaped((RING, length, wide), LOW),
        ],
        ranks,
        gathered,
        *pieces,
        scratch=[pltpu.VMEM((width, lanes), FULL), pltpu.VMEM((8, wide), FULL)],
        first_specs=[
            pl.BlockSpec((parts, rows, lanes), lambda i: (0, 0, 0), memory_space=pltpu.VMEM),
        ],
        flops=2 * RING * length * width * wide,
        moved=16 << 20,
    )


def down_blocks(d, rows, parts):
    z, rest = divmod(d, parts // RING)
    size = parts * rows // RING
    return [(j * size, (rest * RING + j) * rows, z * size) for j in range(RING)]


def run_unpack(ranks, gathered, column, count, is_down):
    parts, rows, unused = gathered.shape
    width = parts * rows
    size = width // RING

    def kernel(ranks_ref, got_ref, *refs):
        work_ref = refs[count]
        for index, ref in enumerate(refs[:count]):
            lane = column + index * width
            for d in range(parts):
                piece = got_ref[d, :, lane : lane + width].astype(FULL)
                if is_down:
                    for at, row, col in down_blocks(d, rows, parts):
                        work_ref[row : row + rows, col : col + size] = piece[:, at : at + size]
                else:
                    work_ref[d * rows : (d + 1) * rows, :] = piece
            ref[...] = work_ref[...].astype(LOW)

    return call(
        kernel,
        [shaped((width, width), LOW)] * count,
        ranks,
        gathered,
        scratch=[pltpu.VMEM((width, width), FULL)],
        flops=0,
        moved=(8 << 20) * count,
    )


def run_mix(ranks, heads, out_low, tokens, vec):
    length, width = tokens.shape

    def kernel(
        ranks_ref, h0, h1, h2, h3, out_ref, token_ref, vec_ref, heads_ref, mixed_ref, two_ref
    ):
        for m, ref in enumerate((h0, h1, h2, h3)):
            source = lax.rem(ranks_ref[0] + m, RING)
            start = pl.multiple_of(source * GROUP, GROUP)
            heads_ref[:, pl.ds(start, GROUP)] = ref[:, :GROUP]

            @pl.when(source == RING - 1)
            def last():
                heads_ref[:, RING * GROUP :] = ref[:, GROUP:]

        mixed = token_ref[...].astype(FULL) + (
            dot(heads_ref[...], out_ref[...]) + vec_ref[4:5, :]
        )
        mixed_ref[...] = mixed
        unit, unused = normed(mixed)
        store_wide(two_ref, unit * vec_ref[5:6, :] + vec_ref[6:7, :])

    return call(
        kernel,
        [
            shaped((length, width), LOW),
            shaped((length, width), FULL),
            shaped((length, lanes_of(width)), LOW),
        ],
        ranks,
        *heads,
        out_low,
        tokens,
        vec,
        flops=2 * length * width * width,
        moved=8 << 20,
    )


def run_d_act(ranks, pieces, down_low):
    length, width = pieces[0].shape[0], down_low.shape[1]

    def kernel(ranks_ref, c0, c1, c2, c3, c4, down_ref, cot_ref, act_ref):
        for ref, first, count in spread_rows((c0, c1, c2, c3, c4)):
            rows = ref[:, :width]
            cot_ref[first : first + count, :] = rows
            act_ref[first : first + count, :] = dot_last(rows, down_ref[...])

    return call(
        kernel,
        [shaped((RING * length, width), LOW), shaped((RING * length, width), FULL)],
        ranks,
        *pieces,
        down_low,
        flops=2 * RING * length * width * width,
        moved=12 << 20,
    )


def run_ffn(ranks, pieces, up_low, d_act, vec):
    length, width = pieces[0].shape[0], up_low.shape[0]

    def kernel(
        ranks_ref, a0, a1, a2, a3, a4, up_ref, d_act_ref, vec_ref,
        two_ref, act_ref, d_pre_ref, own_ref, p1, p2, p3, sums_ref,
    ):
        for ref, first, count in spread_rows((a0, a1, a2, a3, a4)):
            two_ref[first : first + count, :] = ref[:, :width]
        bias = vec_ref[pl.ds(7 + ranks_ref[0], 1), :]
        total = None
        for block, out_ref in enumerate((own_ref, p1, p2, p3)):
            rows = slice(block * length, (block + 1) * length)
            value = dot(two_ref[rows, :], up_ref[...]) + bias
            square = value * value
            bent = jnp.tanh(GELU_SCALE * (value + GELU_CUBIC * value * square))
            half = 0.5 * (1.0 + bent)
            act_ref[rows, :] = (value * half).astype(LOW)
            slope = half + (0.5 * GELU_SCALE) * value * (1.0 - bent * bent) * (
                1.0 + (3.0 * GELU_CUBIC) * square
            )
            d_pre = (slope * d_act_ref[rows, :]).astype(LOW)
            d_pre_ref[rows, :] = d_pre
            part = jnp.sum(d_pre.astype(FULL), axis=0, keepdims=True)
            total = part if total is None else total + part
            store_wide(out_ref, dot_last(d_pre, up_ref[...]))
        sums_ref[...] = jnp.broadcast_to(total, sums_ref.shape)

    return call(
        kernel,
        [shaped((RING * length, width), LOW)] * 3
        + [shaped((length, width), FULL)]
        + [shaped((length, lanes_of(width)), LOW)] * 3
        + [shaped((8, width), FULL)],
        ranks,
        *pieces,
        up_low,
        d_act,
        vec,
        flops=4 * RING * length * width * width,
        moved=24 << 20,
    )


def run_back_two(ranks, mixed, terms, cot, out_low, vec):
    length, width = mixed.shape

    def kernel(
        ranks_ref, mixed_ref, own_ref, p1, p2, p3, cot_ref, out_ref, vec_ref,
        d_mixed_ref, branch_ref, d0, d1, d2, d3, sums_ref, work_ref,
    ):
        d_two = own_ref[...] + (
            p1[:, :width].astype(FULL) + p2[:, :width].astype(FULL) + p3[:, :width].astype(FULL)
        )
        d_inputs, d_gain, d_shift = norm_back(mixed_ref[...], vec_ref[5:6, :], d_two)
        cot_rows = cot_ref[...].astype(FULL)
        d_mixed = cot_rows + d_inputs
        d_mixed_ref[...] = d_mixed
        branch = d_mixed.astype(LOW)
        branch_ref[...] = branch
        sums_ref[0:1, :] = d_gain
        sums_ref[1:2, :] = d_shift
        sums_ref[2:3, :] = jnp.sum(branch.astype(FULL), axis=0, keepdims=True)
        sums_ref[3:4, :] = jnp.sum(cot_rows, axis=0, keepdims=True)
        sums_ref[4:8, :] = jnp.zeros((4, width), FULL)
        work_ref[...] = dot_last(branch, out_ref[...]).astype(LOW)
        for r, ref in enumerate((d0, d1, d2, d3)):
            start = pl.multiple_of(lax.rem(ranks_ref[0] + r, RING) * GROUP, GROUP)
            ref[...] = work_ref[:, pl.ds(start, SPAN)]

    return call(
        kernel,
        [shaped((length, width), FULL), shaped((length, width), LOW)]
        + [shaped((length, SPAN), LOW)] * RING
        + [shaped((8, width), FULL)],
        ranks,
        mixed,
        *terms,
        cot,
        out_low,
        vec,
        scratch=[pltpu.VMEM((length, width), LOW)],
        flops=2 * length * width * width,
        moved=10 << 20,
    )


def run_back_one(ranks, tokens, terms, d_mixed, vec):
    length, width = tokens.shape

    def kernel(ranks_ref, token_ref, own_ref, p1, p2, p3, d_mixed_ref, vec_ref, out_ref, sums_ref):
        d_one = own_ref[...] + (
            p1[:, :width].astype(FULL) + p2[:, :width].astype(FULL) + p3[:, :width].astype(FULL)
        )
        d_inputs, d_gain, d_shift = norm_back(
            token_ref[...].astype(FULL), vec_ref[0:1, :], d_one
        )
        out_ref[...] = d_mixed_ref[...] + d_inputs
        sums_ref[0:1, :] = d_gain
        sums_ref[1:2, :] = d_shift
        sums_ref[2:8, :] = jnp.zeros((6, width), FULL)

    return call(
        kernel,
        [shaped((length, width), FULL), shaped((8, width), FULL)],
        ranks,
        tokens,
        *terms,
        d_mixed,
        vec,
        flops=0,
        moved=6 << 20,
    )


def run_project(ranks, left, right, turned):
    length = left.shape[0] // RING
    width = right.shape[0] if turned else right.shape[1]

    def kernel(ranks_ref, left_ref, right_ref, own_ref, p1, p2, p3):
        for block, out_ref in enumerate((own_ref, p1, p2, p3)):
            rows = left_ref[block * length : (block + 1) * length, :]
            product = dot_last(rows, right_ref[...]) if turned else dot(rows, right_ref[...])
            store_wide(out_ref, product)

    return call(
        kernel,
        [shaped((length, width), FULL)] + [shaped((length, lanes_of(width)), LOW)] * 3,
        ranks,
        left,
        right,
        flops=2 * left.shape[0] * left.shape[1] * width,
        moved=8 << 20,
    )


def run_grads(ranks, two, d_pre, act, cot, rows):
    width = two.shape[1]
    parts = width // rows
    padded = -(-rows // 8) * 8
    strip = width // RING

    def kernel(ranks_ref, two_ref, d_pre_ref, act_ref, cot_ref, out_ref, turned_ref, work_ref):
        out_ref[:, rows:, :] = jnp.zeros((parts, padded - rows, 2 * width), FULL)
        for index, (left, right) in enumerate(((two_ref, d_pre_ref), (act_ref, cot_ref))):
            turned_ref[...] = left[...].T
            for block in range(RING):
                part = slice(block * strip, (block + 1) * strip)
                work_ref[part, :] = dot(turned_ref[part, :], right[...])
            for d in range(parts):
                if index == 0:
                    out_ref[d, :rows, :width] = work_ref[d * rows : (d + 1) * rows, :]
                    continue
                for at, row, col in down_blocks(d, rows, parts):
                    out_ref[d, :rows, width + at : width + at + strip] = work_ref[
                        row : row + rows, col : col + strip
                    ]

    return call(
        kernel,
        [shaped((parts, padded, 2 * width), FULL)],
        ranks,
        two,
        d_pre,
        act,
        cot,
        scratch=[pltpu.VMEM((width, two.shape[0]), LOW), pltpu.VMEM((width, width), FULL)],
        flops=4 * two.shape[0] * width * width,
        moved=32 << 20,
    )[0]


def padded_rows(rows):
    return -(-rows // 8) * 8


def fill_by_core(ranks_ref, work_ref, keep_ref, send_ref, rows):
    parts = work_ref.shape[0] // rows
    for ref in (keep_ref, send_ref):
        ref[:, rows:, :] = jnp.zeros((ref.shape[0], ref.shape[1] - rows, ref.shape[2]), LOW)

    def fill(own_core):
        for d in range(parts):
            ref = keep_ref if d % CORES == own_core else send_ref
            ref[d // CORES, :rows, :] = work_ref[d * rows : (d + 1) * rows, :].astype(LOW)

    @pl.when(ranks_ref[1] == 0)
    def even():
        fill(0)

    @pl.when(ranks_ref[1] == 1)
    def odd():
        fill(1)


def run_grad_out(ranks, heads, pieces, rows):
    width = heads.shape[1]
    size = pieces[0].shape[1]
    lanes = lanes_of(size)
    half = width // rows // CORES

    def kernel(ranks_ref, heads_ref, b0, b1, b2, b3, keep_ref, send_ref, work_ref):
        turned = heads_ref[...].T
        for index, ref in enumerate((b0, b1, b2, b3)):
            first = index * lanes
            work_ref[:, first : first + size] = dot(turned, ref[...])
            work_ref[:, first + size : first + lanes] = jnp.zeros((width, lanes - size), FULL)
        fill_by_core(ranks_ref, work_ref, keep_ref, send_ref, rows)

    return call(
        kernel,
        [shaped((half, padded_rows(rows), RING * lanes), LOW)] * 2,
        ranks,
        heads,
        *pieces,
        scratch=[pltpu.VMEM((width, RING * lanes), FULL)],
        flops=2 * heads.shape[0] * width * width,
        moved=8 << 20,
    )


def run_out_blocks(ranks, keep, came, size):
    half, padded, wide = keep.shape
    lanes = wide // RING
    total = half * padded

    def kernel(ranks_ref, keep_ref, came_ref, *refs):
        for index, ref in enumerate(refs):
            part = slice(index * lanes, (index + 1) * lanes)
            rows = keep_ref[:, :, part].astype(FULL) + came_ref[:, :, part].astype(FULL)
            store_wide(ref, rows.reshape(total, lanes).T[:size])

    return call(
        kernel,
        [shaped((size, lanes_of(total)), FULL)] + [shaped((size, lanes_of(total)), LOW)] * 3,
        ranks,
        keep,
        came,
        flops=0,
        moved=6 << 20,
    )


def run_pack(ranks, one, d_qkv, rows):
    width = one.shape[1]
    wide = d_qkv.shape[1]
    lanes = lanes_of(wide)
    half = width // rows // CORES
    strip = width // RING

    def kernel(ranks_ref, one_ref, grad_ref, keep_ref, send_ref, turned_ref, work_ref):
        turned_ref[...] = one_ref[...].T
        for block in range(RING):
            part = slice(block * strip, (block + 1) * strip)
            work_ref[part, :wide] = dot(turned_ref[part, :], grad_ref[...])
        work_ref[:, wide:] = jnp.zeros((width, lanes - wide), FULL)
        fill_by_core(ranks_ref, work_ref, keep_ref, send_ref, rows)

    return call(
        kernel,
        [shaped((half, padded_rows(rows), lanes), LOW)] * 2,
        ranks,
        one,
        d_qkv,
        scratch=[pltpu.VMEM((width, one.shape[0]), LOW), pltpu.VMEM((width, lanes), FULL)],
        flops=2 * one.shape[0] * width * wide,
        moved=12 << 20,
    )


def run_join(ranks, keep, came, outs, wide, rows, rows_y):
    half, padded, unused = keep.shape
    size = outs[0].shape[0]
    total = half * padded
    lanes = lanes_of(wide + size)

    def kernel(ranks_ref, keep_ref, came_ref, o0, o1, o2, o3, *refs):
        work_ref = refs[rows_y]
        work_ref[:, :, :wide] = keep_ref[:, :, :wide].astype(FULL) + came_ref[
            :, :, :wide
        ].astype(FULL)
        out_sum = (o0[:, :total].astype(FULL) + o1[:, :total].astype(FULL)) + (
            o2[:, :total].astype(FULL) + o3[:, :total].astype(FULL)
        )
        work_ref[:, :, wide : wide + size] = out_sum.T.reshape(half, padded, size)
        work_ref[:, :, wide + size :] = jnp.zeros((half, padded, lanes - wide - size), FULL)
        for r, ref in enumerate(refs[:rows_y]):
            at = lax.rem(ranks_ref[2] + r, rows_y)
            for z in range(RING):
                ref[z] = work_ref[z * rows_y + at, :rows, :].astype(ref.dtype)

    return call(
        kernel,
        [shaped((RING, rows, lanes), FULL)] + [shaped((RING, rows, lanes), LOW)] * (rows_y - 1),
        ranks,
        keep,
        came,
        *outs,
        scratch=[pltpu.VMEM((half, padded, lanes), FULL)],
        flops=0,
        moved=8 << 20,
    )


def run_fold_z(ranks, terms, rows):
    groups, unused, width = terms[0].shape

    def kernel(ranks_ref, *refs):
        ins, outs = refs[: len(terms)], refs[len(terms) :]
        for r, out_ref in enumerate(outs):
            at = lax.rem(ranks_ref[3] + r, RING)
            total = ins[0][at].astype(FULL)
            for ref in ins[1:]:
                total = total + ref[at].astype(FULL)
            out_ref[...] = total.astype(out_ref.dtype)

    return call(
        kernel,
        [shaped((rows, width), FULL)] + [shaped((rows, width), LOW)] * 3,
        ranks,
        *terms,
        flops=0,
        moved=4 << 20,
    )


def run_down(ranks, act, down):
    width = down.shape[1]
    length = act.shape[0] // RING

    def kernel(ranks_ref, act_ref, down_ref, out_ref):
        for block in range(RING):
            at = lax.rem(ranks_ref[0] + block, RING)
            product = dot(act_ref[block * length : (block + 1) * length, :], down_ref[...])
            out_ref[at, :, :width] = product.astype(LOW)
            out_ref[at, :, width:] = jnp.zeros((length, lanes_of(width) - width), LOW)

    return call(
        kernel,
        [shaped((RING, length, lanes_of(width)), LOW)],
        ranks,
        act,
        down,
        flops=2 * act.shape[0] * act.shape[1] * width,
        moved=8 << 20,
    )[0]


def after(item, *others):
    return lax.optimization_barrier((item,) + others)[0]


def permute(item, axes, pairs):
    return lax.ppermute(item, axes, pairs)


def ctx_shift(item, step):
    return permute(item, "ctx", [(i, (i + step) % RING) for i in range(RING)])


def gather_pieces(item, *between):
    half = item.shape[0] // 2
    left = ctx_shift(item, 1)
    right = ctx_shift(item, 3)
    left, right = lax.optimization_barrier((left, right) + between)[:2]
    top = ctx_shift(left[:half], 1)
    bottom = ctx_shift(right[half:], 3)
    return (item, right, top, bottom, left)


def gather_small(item):
    return jnp.stack([item, ctx_shift(item, 3), ctx_shift(item, 2), ctx_shift(item, 1)])


def to_global(relative, rank):
    doubled = jnp.concatenate([relative, relative[: RING - 1]], axis=0)
    return lax.dynamic_slice_in_dim(doubled, lax.rem(RING - rank, RING), RING, axis=0)


def exchange(pieces):
    return [pieces[0]] + [ctx_shift(pieces[RING - r], RING - r) for r in (1, 2, 3)]


def send_on(pieces):
    return [pieces[0]] + [ctx_shift(pieces[r], r) for r in (1, 2, 3)]


def dp_perm(dp_count, move):
    rows = dp_count // (RING * CORES)
    pairs = []
    for z in range(RING):
        for y in range(rows):
            for core in range(CORES):
                to_z, to_y, to_core = move(z, y, core, rows)
                pairs.append(((z * rows + y) * CORES + core, (to_z * rows + to_y) * CORES + to_core))
    return pairs


def swap_core(item, dp_count):
    return permute(
        item, "dp", dp_perm(dp_count, lambda z, y, core, rows: (z, y, 1 - core))
    )


def send_axis(pieces, axis, dp_count):
    came = [pieces[0]]
    for step, piece in enumerate(pieces[1:], 1):
        if axis == "z":
            perm = dp_perm(dp_count, lambda z, y, core, rows: ((z + step) % RING, y, core))
        else:
            perm = dp_perm(dp_count, lambda z, y, core, rows: (z, (y + step) % rows, core))
        came.append(permute(piece, "dp", perm))
    return came


def sum_everywhere(item, dp_count, beside):
    rows = dp_count // (RING * CORES)
    item = item + swap_core(item, dp_count)
    for name in ("y", "z", "x"):
        if name == "x":
            item, *beside = lax.optimization_barrier((item,) + tuple(beside))
        parts = [item]
        for step in (1, 2, 3):
            if name == "x":
                perm = [(i, i ^ step) for i in range(RING)]
                parts.append(lax.ppermute(item, "ctx", perm))
            elif name == "z":
                perm = dp_perm(dp_count, lambda z, y, core, rows: (z ^ step, y, core))
                parts.append(lax.ppermute(item, "dp", perm))
            elif rows == RING:
                perm = dp_perm(dp_count, lambda z, y, core, rows: (z, y ^ step, core))
                parts.append(lax.ppermute(item, "dp", perm))
        if len(parts) == RING:
            item = (parts[0] + parts[1]) + (parts[2] + parts[3])
    return item, *beside


def plane_pairs(dp_count):
    inner = dp_count // RING
    return [
        ((z * inner + rest) * RING + x, (x * inner + rest) * RING + z)
        for z in range(RING)
        for rest in range(inner)
        for x in range(RING)
    ]


def in_columns(item, rows):
    return jnp.concatenate(
        [item[first : first + rows] for first in range(0, item.shape[0], rows)], axis=1
    )


def body(
    tokens,
    cotangent,
    positions,
    w_qkv,
    w_out,
    w_up,
    w_down,
    vectors,
    moment_qkv,
    square_qkv,
    moment_out,
    square_out,
    moment_up,
    square_up,
    moment_down,
    square_down,
    moment_vec,
    square_vec,
):
    unused, local_len, width = tokens.shape
    dp_count = lax.axis_size("dp")
    rows_y = dp_count // (RING * CORES)
    rank = lax.axis_index("ctx")
    dp_rank = lax.axis_index("dp")
    rank_core = lax.rem(dp_rank, CORES)
    rank_y = lax.rem(lax.div(dp_rank, CORES), rows_y)
    rank_z = lax.div(dp_rank, CORES * rows_y)
    ranks = jnp.stack([rank, rank_core, rank_y, rank_z]).astype(jnp.int32)
    row_size = w_qkv.shape[0]
    full_len = local_len * RING

    shard_cols = jnp.concatenate(
        [w_qkv.astype(LOW), w_out.astype(LOW), vectors.astype(LOW)], axis=1
    )
    gathered = to_global(gather_small(shard_cols), rank)
    qkv_size, out_size = w_qkv.shape[1], w_out.shape[1]
    qkv_rows = jnp.concatenate([gathered[s, :, :qkv_size] for s in range(RING)], axis=1)
    out_rows = jnp.concatenate(
        [gathered[s, :, qkv_size : qkv_size + out_size] for s in range(RING)], axis=1
    )
    vec_rows = jnp.concatenate([gathered[s, :, qkv_size + out_size :] for s in range(RING)], axis=1)
    head_start = rank * GROUP
    qkv_own = [
        lax.dynamic_slice_in_dim(qkv_rows[:, part * width : (part + 1) * width], head_start, SPAN, 1)
        for part in range(3)
    ]
    vec_wide = jnp.pad(vec_rows, ((0, 0), (0, 1024 - 3 * SPAN - vec_rows.shape[1])))
    weights_all = lax.all_gather(
        jnp.concatenate(qkv_own + [vec_wide, out_rows, w_up.astype(LOW)], axis=1),
        "dp",
        axis=0,
        tiled=False,
    )
    token_low = tokens.reshape(local_len, width)
    cot_low = cotangent.reshape(local_len, width)
    lane_fill = ((0, 0), (0, lanes_of(width) - width))
    token_pieces = gather_pieces(jnp.pad(token_low, lane_fill))
    pos_seq = gather_small(after(positions, *token_pieces))

    down_swapped = permute(
        after(w_down.astype(LOW), *token_pieces), ("dp", "ctx"), plane_pairs(dp_count)
    )
    down_all = lax.all_gather(
        in_columns(down_swapped, row_size), "dp", axis=0, tiled=False
    )

    qkv_low, vec, a_one, qkv_blocks = run_enter(
        ranks, after(weights_all, pos_seq), token_pieces
    )
    *heads_pieces, lse = run_forward(ranks, pos_seq, qkv_blocks)
    cot_pieces = gather_pieces(
        after(jnp.pad(cot_low, lane_fill), down_swapped, pos_seq), *heads_pieces
    )
    out_low, up_low = run_unpack(ranks, weights_all, 1024, 2, False)
    (down_low,) = run_unpack(ranks, down_all, 0, 1, True)
    heads_came = exchange(heads_pieces)
    heads_low, mixed, a_two = run_mix(
        ranks, heads_came, after(out_low, *cot_pieces), token_low, vec
    )
    cot_seq, d_act = run_d_act(ranks, cot_pieces, down_low)
    two_pieces = gather_pieces(a_two, d_act)
    a_two_seq, act_low, d_pre, own_two, p1, p2, p3, d_pre_sums = run_ffn(
        ranks, two_pieces, up_low, d_act, vec
    )
    d_two_terms = send_on([own_two, p1, p2, p3])

    grads_two = run_grads(ranks, a_two_seq, d_pre, act_low, cot_seq, row_size)
    down_rows = run_down(ranks, after(act_low, grads_two), down_low)
    gate = lax.optimization_barrier(tuple(d_two_terms) + (grads_two, down_rows))
    d_two_terms = gate[:4]
    grads_two, down_rows = gate[4:]
    summed_two = lax.psum_scatter(
        grads_two.reshape(dp_count * grads_two.shape[1], 2 * width),
        "dp",
        scatter_dimension=0,
        tiled=True,
    )
    summed_two = lax.optimization_barrier(summed_two)
    grad_up = summed_two[:row_size, :width]
    grad_down_rows = summed_two[:row_size, width:]

    d_mixed, d_branch, g0, g1, g2, g3, sums_two = run_back_two(
        ranks, mixed, d_two_terms, cot_low, out_low, vec
    )
    d_heads_came = exchange([g0, g1, g2, g3])
    out_keep, out_send = run_grad_out(
        ranks,
        heads_low,
        [
            lax.dynamic_slice_in_dim(d_branch, lax.rem(rank + r, RING) * out_size, out_size, 1)
            for r in range(RING)
        ],
        row_size,
    )
    out_blocks = run_out_blocks(ranks, out_keep, swap_core(out_send, dp_count), out_size)
    gate = lax.optimization_barrier(tuple(d_heads_came) + tuple(out_blocks))
    d_heads_came = gate[:4]
    out_came = send_on(gate[4:])
    d_qkv_blocks = run_backward(ranks, pos_seq, qkv_blocks, d_heads_came, lse)
    gate = lax.optimization_barrier((d_qkv_blocks,) + tuple(out_came))
    d_qkv = gate[0].reshape(full_len, 3 * SPAN)
    out_came = gate[1:]
    qkv_keep, qkv_send = run_pack(ranks, a_one, d_qkv, row_size)
    qkv_came = swap_core(qkv_send, dp_count)
    one_pieces = run_project(ranks, after(d_qkv, qkv_keep), qkv_low, True)
    d_one_terms = send_on(one_pieces)
    qkv_came = after(qkv_came, *one_pieces)
    parts = run_join(ranks, qkv_keep, qkv_came, out_came, 3 * SPAN, row_size, rows_y)
    gate = lax.optimization_barrier(tuple(send_axis(parts, "y", dp_count)) + tuple(d_one_terms))
    parts = run_fold_z(ranks, gate[:rows_y], row_size)
    d_one_terms = gate[rows_y:]
    down_rows = after(down_rows, summed_two, *d_one_terms)
    down_sum = lax.psum_scatter(
        down_rows.reshape(full_len, down_rows.shape[2]), "ctx", scatter_dimension=0, tiled=True
    )
    down_sum = lax.optimization_barrier(down_sum)[:, :width].astype(FULL)
    d_token_rows, sums_one = run_back_one(ranks, token_low, d_one_terms, d_mixed, vec)
    d_tokens = d_token_rows.reshape(tokens.shape)
    came = send_axis(parts, "z", dp_count)
    grad_last = came[0] + (came[1].astype(FULL) + came[2].astype(FULL) + came[3].astype(FULL))
    grad_qkv_own = grad_last[:, : 3 * SPAN]
    grad_out = grad_last[:, 3 * SPAN : 3 * SPAN + out_size]

    grad_down = permute(
        jnp.concatenate(
            [grad_down_rows[:, c * out_size : (c + 1) * out_size] for c in range(RING)], axis=0
        ),
        ("dp", "ctx"),
        plane_pairs(dp_count),
    )
    d_qkv_sums = jnp.sum(d_qkv.astype(FULL), axis=0)
    empty = jnp.zeros((width,), FULL)
    vec_terms = jnp.stack(
        [
            sums_one[0],
            sums_one[1],
            lax.dynamic_update_slice(empty, d_qkv_sums[:SPAN], (head_start,)),
            lax.dynamic_update_slice(empty, d_qkv_sums[2 * SPAN :], (head_start,)),
            sums_two[2],
            sums_two[0],
            sums_two[1],
        ]
        + [jnp.where(rank == c, d_pre_sums[0], 0.0) for c in range(RING)]
        + [sums_two[3]],
        axis=0,
    )
    local_sq = (
        jnp.sum(grad_qkv_own * grad_qkv_own)
        + jnp.sum(grad_out * grad_out)
        + jnp.sum(grad_up * grad_up)
        + jnp.sum(grad_down_rows * grad_down_rows)
    )
    vec_count = vec_terms.shape[0]
    first_lane = lax.broadcasted_iota(jnp.int32, (4, width), 1) == 0
    first_row = lax.broadcasted_iota(jnp.int32, (4, width), 0) == 0
    payload = jnp.concatenate(
        [vec_terms, jnp.where(first_lane & first_row, local_sq, 0.0)], axis=0
    )
    qkv_near = gather_small(grad_qkv_own)
    payload, qkv_near, grad_down, down_sum = sum_everywhere(
        payload, dp_count, (qkv_near, grad_down, down_sum)
    )
    vec_total = payload[:vec_count]
    outputs = (mixed + (down_sum + vec[11])).astype(LOW).reshape(tokens.shape)
    total_sq = payload[vec_count, 0] + jnp.sum(vec_total * vec_total)
    grad_norm = jnp.sqrt(total_sq)
    clip_factor = CLIP_LIMIT / jnp.maximum(grad_norm, CLIP_LIMIT)

    col_size = vec_count // RING
    grad_vec = lax.dynamic_slice(
        vec_total, (rank * col_size, dp_rank * row_size), (col_size, row_size)
    ).T
    qkv_groups = to_global(qkv_near, rank)
    grad_qkv_rows = jnp.concatenate(
        [
            qkv_groups[s, :, part * SPAN : part * SPAN + (SPAN if s == RING - 1 else GROUP)]
            for part in range(3)
            for s in range(RING)
        ],
        axis=1,
    )
    grad_qkv = lax.dynamic_slice_in_dim(grad_qkv_rows, rank * qkv_size, qkv_size, 1)

    first_qkv, second_qkv, updated_qkv = adam_step(
        w_qkv, moment_qkv, square_qkv, grad_qkv * clip_factor, LEARN_RATES[0], WEIGHT_DECAYS[0]
    )
    first_out, second_out, updated_out = adam_step(
        w_out, moment_out, square_out, grad_out * clip_factor, LEARN_RATES[1], WEIGHT_DECAYS[1]
    )
    first_up, second_up, updated_up = adam_step(
        w_up, moment_up, square_up, grad_up * clip_factor, LEARN_RATES[2], WEIGHT_DECAYS[2]
    )
    first_down, second_down, updated_down = adam_step(
        w_down, moment_down, square_down, grad_down * clip_factor, LEARN_RATES[3], WEIGHT_DECAYS[3]
    )
    first_vec, second_vec, updated_vec = adam_step(
        vectors, moment_vec, square_vec, grad_vec * clip_factor, LEARN_RATES[4], WEIGHT_DECAYS[4]
    )
    return (
        outputs,
        d_tokens,
        grad_norm,
        first_qkv,
        second_qkv,
        updated_qkv,
        first_out,
        second_out,
        updated_out,
        first_up,
        second_up,
        updated_up,
        first_down,
        second_down,
        updated_down,
        first_vec,
        second_vec,
        updated_vec,
    )


def solution(mesh):
    token_spec = P("dp", "ctx", None)
    flat_spec = P("dp", "ctx")
    return jax.shard_map(
        body,
        mesh=mesh,
        in_specs=(token_spec, token_spec) + (flat_spec,) * 16,
        out_specs=(token_spec, token_spec, P()) + (flat_spec,) * 15,
        check_vma=False,
    )
```
